32 devices in a mesh: rack: 8 (over y, x, core), expert: 4 (over z).
Axes of the slice: x: 2, y: 2, z: 4, core: 2. Of those that a mesh axis runs over, the one named last changes fastest.
Arguments:
- hidden_in: bfloat16 [32, 3584], P(('rack', 'expert')), may hold values from -6 to 6
- norm_gain: float32 [3584], replicated, may hold values from 0.1 to 1.9
- expert_ids: int32 [4, 32, 8], P(None, ('rack', 'expert')), may hold values from 0 to 7, all different within a row; in each aligned block of 4 rows (0 to 3, 4 to 7, ..., all dimensions but the last counted through in order) at most 4 rows name the same one
- gate_levels: int32 [4, 32, 8], P(None, ('rack', 'expert')), may hold values from 1 to 255
- w_gate_up: bfloat16 [8, 4, 1792, 2, 1024], P('rack', 'expert'), may hold values from -0.09375 to 0.09375
- w_down: bfloat16 [8, 4, 1024, 1792], P('rack', 'expert'), may hold values from -0.125 to 0.125
Outputs:
- hidden_out: float32 [32, 3584], P(('rack', 'expert'))
The draws below stay inside these ranges and needn't reach their ends.
Inputs may be any that keep to these rules, and one draw needn't show every extreme that they name: `expert_ids`: each token names 8 different experts in each step; in each step at most 4 of the 4 tokens of one index of rack (an aligned block of the token order) name the same expert, and that many do in some blocks.
All inputs are finite; a program needn't handle non-finite values.
Results may differ from the reference program's by a relative error of at most 0.015.
Values may be sent and summed in bfloat16 or wider, within the bound.
No kernel may reach another device: no remote copies, remote signals or barrier semaphores. Data moves between devices by JAX's collectives and lax.ppermute only.
A program may use at most 64 MiB of HBM per device.

```python
import math
import jax
import jax.numpy as jnp
import numpy as np
from jax import lax

D = 3584
HID = 2048
TOP = 8
STEPS = 4
TOK_DEV = 1
EXPERTS = 8
HPART = 1024
RACK_ROWS = 4
TOKENS = 32
CAP = 4
N_RACK = 8
N_EXPERT = 4


def touch_ends(entries, key, smallest, high):
    longest = entries.shape.index(max(entries.shape))
    spots = []
    for shift in (0, 1):
        where = [jax.random.randint(jax.random.fold_in(key, axis), (), 0, length) for axis, length in enumerate(entries.shape)]
        where[longest] = (where[longest] + shift) % entries.shape[longest]
        spots.append(tuple(where))
    return entries.at[spots[0]].set(smallest).at[spots[1]].set(high)


def block_levels(own_key, shape, split, least, largest):
    def one(axis_at, parts):
        steps = jax.random.uniform(jax.random.fold_in(jax.random.fold_in(own_key, 6), axis_at), (parts,), jnp.float32, least / len(split), largest / len(split))
        return jnp.repeat(jnp.exp(steps), shape[axis_at] // parts).reshape((-1,) + (1,) * (len(shape) - axis_at - 1))

    loudness = one(*split[0])
    for cut in split[1:]:
        loudness = loudness * one(*cut)
    return loudness


def routed_block(own_key, own, number, rows, number_of, top, most, skew):
    ranking = jax.random.permutation(own_key, number_of)
    crowded, ordinary = portions_of(number_of, rows * top, most, skew, True), portions_of(number_of, rows * top, most, skew, False)
    places = jnp.arange(number_of)

    def named(tallies, rotation):
        used = int((tallies > 0).sum())
        fixed = max(1, used // 4)
        moved = fixed + (places - fixed + rotation * (used - fixed)) % max(1, number_of - fixed)
        return jnp.zeros((number_of,), jnp.int32).at[ranking[jnp.where(places < fixed, places, moved)]].set(jnp.asarray(tallies, jnp.int32))

    tallies = jnp.where(number % 4 == 0, named(crowded, number // 4), named(ordinary, number - number // 4 - 1))
    mixed = jax.random.permutation(jax.random.fold_in(own, 3), number_of)
    donor, taker = mixed[0:number_of // 2 * 2:2], mixed[1:number_of // 2 * 2:2]
    room = jnp.minimum(tallies[donor] - 1, most - tallies[taker]) // 2
    room = jnp.where((donor == ranking[0]) | (taker == ranking[0]) | (tallies[taker] == 0), 0, jnp.maximum(room, 0))
    moved = jax.random.randint(jax.random.fold_in(own, 4), (number_of // 2,), 0, 1 << 20) % (room + 1)
    tallies = tallies.at[donor].add(-moved).at[taker].add(moved)
    items = jnp.searchsorted(jnp.cumsum(tallies), jnp.arange(rows * top), side="right").astype(jnp.int32)
    grid = items.reshape(top, rows).T
    grid = grid[jax.random.permutation(jax.random.fold_in(own, 1), rows)]
    rotation = jax.random.randint(jax.random.fold_in(own, 2), (rows, 1), 0, top)
    return jnp.take_along_axis(grid, (jnp.arange(top)[None, :] + rotation) % top, axis=1)


def portions_of(count, total, most, lean, full):
    loads = [(1 << 20) // math.isqrt(rank ** lean) + 1 for rank in range(1, count + 1)]
    largest = most if full else min(most, max(-(-total // count), total * loads[0] // sum(loads)))
    least = 1 if total - largest >= count - 1 else 0
    counts, spare = [largest] + [least] * (count - 1), total - largest - least * (count - 1)
    while spare > 0:
        movable = [i for i in range(1, count) if counts[i] < largest] or [i for i in range(1, count) if counts[i] < most]
        mass, left = sum([loads[i] for i in movable]), spare
        for i in movable:
            extra = min(most - counts[i], max(1, left * loads[i] // mass), spare)
            counts[i] = counts[i] + extra
            spare = spare - extra
    return np.array(counts)


def normal_values(key, shape, width, reach, pieces=(), kind=jnp.bfloat16):
    factor_of = block_levels(key, shape, pieces, -0.22, 0.18) if pieces else 1.0
    array = jax.random.normal(key, shape, jnp.float32) * width * factor_of
    return jnp.minimum(jnp.maximum(array, -reach), reach).astype(kind)


def setup_inputs(seed: int = 0) -> dict:
    streams_of = jax.random.split(jax.random.key(seed), 7)
    hidden_in = normal_values(streams_of[0], (TOKENS, D), 1.0, 6.0, ((0, 32),))
    norm_gain = jnp.clip(1.0 + 0.18 * jax.random.normal(streams_of[1], (D,), jnp.float32), 0.1, 1.9)
    expert_ids_keys = jax.random.split(jax.random.fold_in(streams_of[2], 1), STEPS * TOKENS // RACK_ROWS)
    expert_ids_turns = jax.random.permutation(jax.random.fold_in(streams_of[2], 3), STEPS * TOKENS // RACK_ROWS)
    expert_ids = jax.vmap(lambda own, number: routed_block(jax.random.fold_in(streams_of[2], 2), own, number, RACK_ROWS, EXPERTS, TOP, CAP, 2))(expert_ids_keys, expert_ids_turns).reshape((STEPS, TOKENS, TOP))
    gate_levels = touch_ends(jax.random.randint(streams_of[3], (STEPS, TOKENS, TOP), 1, 256), jax.random.fold_in(streams_of[3], 1), 1, 255).astype(jnp.int32)
    w_gate_up = normal_values(streams_of[4], (EXPERTS, N_EXPERT, D // 2, 2, HPART), D ** -0.5, 0.09375, ((0, 8), (1, 4)))
    w_down = normal_values(streams_of[5], (EXPERTS, N_EXPERT, HPART, D // 2), HID ** -0.5, 0.125, ((0, 8), (1, 4)))
    return {"hidden_in": hidden_in, "norm_gain": norm_gain, "expert_ids": expert_ids, "gate_levels": gate_levels, "w_gate_up": w_gate_up, "w_down": w_down}


def reference(hidden_in, norm_gain, expert_ids, gate_levels, w_gate_up, w_down):
    residual = hidden_in.astype(jnp.float32)
    rack_rows = TOK_DEV * N_EXPERT
    group_total = N_EXPERT // 2
    half_width = D // 2
    token_ids = jnp.arange(TOKENS, dtype=jnp.int32).reshape(N_RACK, rack_rows)
    slot_ids = jnp.arange(CAP, dtype=jnp.int32)
    expert_range = jnp.arange(EXPERTS, dtype=jnp.int32)
    for step_index in range(STEPS):
        mean_square = lax.optimization_barrier(jnp.mean(residual * residual, axis=-1, keepdims=True))
        normed = (residual * lax.rsqrt(mean_square + 1e-06) * norm_gain).astype(jnp.bfloat16)
        picked = expert_ids[step_index]
        level_vals = gate_levels[step_index].astype(jnp.float32)
        shares = level_vals / lax.optimization_barrier(jnp.sum(level_vals, axis=-1, keepdims=True))
        matches = picked[:, :, None] == expert_range[None, None, :]
        chosen = lax.optimization_barrier(jnp.sum(matches.astype(jnp.int32), axis=1))
        mixing = lax.optimization_barrier(jnp.sum(jnp.where(matches, shares[:, :, None], jnp.float32(0.0)), axis=1)).astype(jnp.bfloat16)
        mixing = lax.optimization_barrier(mixing).astype(jnp.float32)
        per_rack = chosen.reshape(N_RACK, rack_rows, EXPERTS)
        slot_rank = jnp.cumsum(per_rack, axis=1) - per_rack
        placement = per_rack[..., None] * (slot_rank[..., None] == slot_ids).astype(jnp.int32)
        token_index = lax.optimization_barrier(jnp.sum(placement * token_ids[:, :, None, None], axis=1))
        valid_rows = lax.optimization_barrier(jnp.sum(placement, axis=1))
        token_index = jnp.transpose(token_index, (1, 0, 2)).reshape(EXPERTS, N_RACK * CAP).astype(jnp.int32)
        valid_rows = jnp.transpose(valid_rows, (1, 0, 2)).reshape(EXPERTS, N_RACK * CAP)

        def expert_term(packed):
            expert_id, row_index, row_valid = packed
            slot_rows = normed[row_index] * row_valid[:, None].astype(jnp.bfloat16)
            gate_up_parts = w_gate_up[expert_id].reshape(group_total, 2, half_width, 2, HPART)
            gate_up_full = jnp.transpose(gate_up_parts, (1, 2, 3, 0, 4)).reshape(D, 2 * HID)
            gate_up = jnp.dot(slot_rows, gate_up_full, preferred_element_type=jnp.float32)
            activated = (jax.nn.silu(gate_up[:, :HID]) * gate_up[:, HID:]).astype(jnp.bfloat16)
            down_parts = w_down[expert_id].reshape(group_total, 2, HPART, half_width)
            down_full = jnp.transpose(down_parts, (0, 2, 1, 3)).reshape(group_total, HPART, D)
            partial_value = jnp.einsum('ngh,ghd->ngd', activated.reshape(-1, group_total, HPART).astype(jnp.float32), down_full.astype(jnp.float32))
            rounded = lax.optimization_barrier(partial_value.astype(jnp.bfloat16))
            return lax.optimization_barrier(jnp.sum(rounded.astype(jnp.float32), axis=1))
        outputs = lax.map(expert_term, (expert_range, token_index, valid_rows))
        slot_weight = mixing[token_index, expert_range[:, None]] * valid_rows.astype(jnp.float32)
        update = jax.ops.segment_sum((outputs * slot_weight[:, :, None]).reshape(-1, D), token_index.reshape(-1), num_segments=TOKENS)
        residual = residual + update
    return residual
```

```python
import jax
import jax.numpy as jnp
from jax import lax
from jax.sharding import PartitionSpec as P

TOP = 8
STEPS = 4


def swapped(shard, axis, bit):
    return lax.ppermute(shard, axis, [(i, i ^ 1 << bit) for i in range(lax.axis_size(axis))])


def exchanged(shard, axis, mask):
    return lax.ppermute(shard, axis, [(i, i ^ mask) for i in range(lax.axis_size(axis))])


def widened(values):
    return values.astype(jnp.float32)


def rounded(values):
    return values.astype(jnp.bfloat16)


def dense_steps(hidden_in, norm_gain, expert_ids, gate_levels, w_gate_up, w_down):
    rack_count = lax.axis_size("rack")
    group_count = lax.axis_size("expert")
    rack_index = lax.axis_index("rack")
    group_index = lax.axis_index("expert")
    chip_count = rack_count // 2
    core_rows = chip_count * group_count
    token_count = 2 * core_rows
    model_width = hidden_in.shape[1]
    half_width = model_width // 2
    part_width = w_down.shape[2]
    first_half = group_index % 2 == 0
    gate_up_weight = w_gate_up[0, 0].reshape(half_width, 2 * part_width)
    down_weight = w_down[0, 0]

    def half_of(rows, own):
        return jnp.where(first_half == own, rows[:, :half_width], rows[:, half_width:])

    gain_half = half_of(norm_gain[None, :], True)

    level_vals = gate_levels[:, 0, :].astype(jnp.float32)
    shares = level_vals / jnp.sum(level_vals, axis=-1, keepdims=True)
    matches = expert_ids[:, 0, :, None] == jnp.arange(rack_count, dtype=jnp.int32)
    own_mixing = rounded(jnp.sum(jnp.where(matches, shares[:, :, None], jnp.float32(0.0)), axis=1))
    own_mixing = own_mixing.reshape(1, STEPS * rack_count)
    mixing_width = -(-STEPS * rack_count // 128) * 128
    own_mixing = jnp.pad(own_mixing, ((0, 0), (0, mixing_width - STEPS * rack_count)))

    rows = jnp.concatenate([half_of(hidden_in, True), own_mixing], axis=1)
    other = jnp.concatenate([half_of(hidden_in, False), own_mixing], axis=1)
    rows = jnp.concatenate([rows, exchanged(other, "expert", 1)], axis=0)
    rows = jnp.concatenate(
        [rows] + [exchanged(rows, "expert", mask) for mask in range(2, group_count, 2)], axis=0
    )
    rows = jnp.concatenate(
        [rows] + [exchanged(rows, "rack", mask) for mask in range(2, rack_count, 2)], axis=0
    )
    rows = jnp.concatenate([rows, exchanged(rows, "rack", 1)], axis=0)
    own_place = rack_index // 2 * group_count + group_index
    places = jnp.arange(token_count, dtype=jnp.int32)
    to_absolute = rounded(places[:, None] == (places[None, :] ^ own_place))
    rows = jnp.dot(to_absolute, rows, preferred_element_type=jnp.float32)
    residual = rows[:, :half_width]
    all_mixing = rows[:, half_width : half_width + STEPS * rack_count]
    own_expert = jnp.arange(rack_count, dtype=jnp.int32) == rack_index
    mixing = jnp.sum(
        jnp.where(own_expert, all_mixing.reshape(token_count, STEPS, rack_count), 0.0), axis=2
    )

    for step_index in range(STEPS):
        last = step_index == STEPS - 1
        square_sum = jnp.sum(residual * residual, axis=1, keepdims=True)
        scaled = rounded(residual * gain_half)
        gate_up = jnp.dot(scaled, gate_up_weight, preferred_element_type=jnp.float32)
        square_high = rounded(lax.reduce_precision(square_sum, 8, 7))
        square_low = rounded(square_sum - lax.reduce_precision(square_sum, 8, 7))
        lane = lax.broadcasted_iota(jnp.int32, (token_count, 128), 1)
        tail = jnp.where(lane == 0, square_high, square_low)
        swapped_rows = exchanged(
            jnp.concatenate([rounded(gate_up), tail], axis=1), "expert", 1
        )
        gate_up = gate_up + widened(swapped_rows[:, : 2 * part_width])
        other_sum = widened(swapped_rows[:, 2 * part_width : 2 * part_width + 1]) + widened(
            swapped_rows[:, 2 * part_width + 1 : 2 * part_width + 2]
        )
        gate_up = gate_up * lax.rsqrt((square_sum + other_sum) / model_width + 1e-06)
        activated = rounded(jax.nn.silu(gate_up[:, :part_width]) * gate_up[:, part_width:])
        term = rounded(jnp.dot(activated, down_weight, preferred_element_type=jnp.float32))
        update = widened(term) * mixing[:, step_index : step_index + 1]
        if last:
            break
        update = update[:core_rows] + widened(exchanged(rounded(update[core_rows:]), "rack", 1))
        sent = rounded(update)
        update = widened(sent)
        for mask in range(2, rack_count, 2):
            update = update + widened(exchanged(sent, "rack", mask))
        sent = rounded(update)
        update = widened(sent)
        for mask in range(2, group_count, 2):
            update = update + widened(exchanged(sent, "expert", mask))
        sent = rounded(update)
        update = jnp.concatenate([sent, exchanged(sent, "rack", 1)], axis=0)
        residual = residual + widened(update)

    token_ids = jnp.arange(token_count, dtype=jnp.int32)
    token_rack = token_ids // group_count
    place_of_token = (
        (token_rack % 2 ^ rack_index % 2) * core_rows
        + token_rack // 2 * group_count
        + token_ids % group_count
    )
    to_tokens = rounded(place_of_token[:, None] == places[None, :])
    outgoing = rounded(
        jnp.dot(to_tokens, rounded(update), preferred_element_type=jnp.float32)
    )
    arrived = lax.all_to_all(outgoing, ("rack", "expert"), split_axis=0, concat_axis=0, tiled=True)
    arrived = widened(arrived)
    is_first = token_ids[:, None] % 2 == 0
    update = jnp.concatenate(
        [
            jnp.sum(jnp.where(is_first, arrived, 0.0), axis=0, keepdims=True),
            jnp.sum(jnp.where(is_first, 0.0, arrived), axis=0, keepdims=True),
        ],
        axis=1,
    )
    own_row = jnp.sum(jnp.where(places[:, None] == own_place, residual, 0.0), axis=0, keepdims=True)
    other_row = jnp.sum(
        jnp.where(places[:, None] == (own_place ^ 1), residual, 0.0), axis=0, keepdims=True
    )
    other_row = exchanged(other_row, "expert", 1)
    own_residual = jnp.where(
        first_half,
        jnp.concatenate([own_row, other_row], axis=1),
        jnp.concatenate([other_row, own_row], axis=1),
    )
    return own_residual + update


def per_device(hidden_in, norm_gain, expert_ids, gate_levels, w_gate_up, w_down):
    rack_count = lax.axis_size("rack")
    group_count = lax.axis_size("expert")
    group_index = lax.axis_index("expert")
    half_index = group_index % 2
    tok_rows = hidden_in.shape[0]
    rack_rows = tok_rows * group_count
    slot_count = min(rack_rows, 3 * rack_rows * TOP // (2 * rack_count))
    model_width = hidden_in.shape[1]
    half_width = model_width // 2
    part_width = w_down.shape[2]
    gate_up_weight = w_gate_up[0, 0].reshape(half_width, 2 * part_width)
    down_weight = w_down[0, 0]
    all_ids, all_levels = (
        lax.all_gather(expert_ids, "expert", axis=1, tiled=True),
        lax.all_gather(gate_levels, "expert", axis=1, tiled=True),
    )
    expert_range = jnp.arange(rack_count, dtype=jnp.int32)
    slot_ids = jnp.arange(slot_count, dtype=jnp.int32)
    residual = hidden_in.astype(jnp.float32)
    for step_index in range(STEPS):
        mean_square = jnp.mean(residual * residual, axis=-1, keepdims=True)
        normed = (residual * lax.rsqrt(mean_square + 1e-06) * norm_gain).astype(jnp.bfloat16)
        rack_normed = lax.all_gather(normed, "expert", axis=0, tiled=True)
        picked = all_ids[step_index]
        level_vals = all_levels[step_index].astype(jnp.float32)
        shares = level_vals / jnp.sum(level_vals, axis=-1, keepdims=True)
        matches = picked[:, :, None] == expert_range[None, None, :]
        chosen = jnp.sum(matches.astype(jnp.int32), axis=1)
        mixing = jnp.sum(jnp.where(matches, shares[:, :, None], jnp.float32(0.0)), axis=1).astype(
            jnp.bfloat16
        )
        slot_rank = jnp.cumsum(chosen, axis=0) - chosen
        placement = chosen[:, :, None] * (slot_rank[:, :, None] == slot_ids).astype(jnp.int32)
        dispatch_map = (
            jnp.transpose(placement, (1, 2, 0))
            .reshape(rack_count * slot_count, rack_rows)
            .astype(jnp.bfloat16)
        )
        outgoing = jnp.dot(dispatch_map, rack_normed, preferred_element_type=jnp.float32).astype(
            jnp.bfloat16
        )
        outgoing = outgoing.reshape(rack_count, slot_count, model_width)
        combine_map = (placement.astype(jnp.bfloat16) * mixing[:, :, None]).reshape(
            rack_rows, rack_count * slot_count
        )
        half_rows = lax.dynamic_slice_in_dim(outgoing, half_index * half_width, half_width, 2)
        slot_rows = lax.all_to_all(half_rows, "rack", split_axis=0, concat_axis=0, tiled=True)
        layout = slot_rows.shape
        flat_rows = slot_rows.reshape(-1, half_width)
        gate_up = jnp.dot(flat_rows, gate_up_weight, preferred_element_type=jnp.float32)
        gate_up = gate_up + swapped(gate_up.astype(jnp.bfloat16), "expert", 0).astype(gate_up.dtype)
        activated = (jax.nn.silu(gate_up[:, :part_width]) * gate_up[:, part_width:]).astype(
            jnp.bfloat16
        )
        partial_value = jnp.dot(activated, down_weight, preferred_element_type=jnp.float32).astype(
            jnp.bfloat16
        )
        partial_value = partial_value.reshape(layout)
        finished = lax.all_to_all(partial_value, "rack", split_axis=0, concat_axis=0, tiled=True)
        partial_sum = jnp.dot(
            combine_map, finished.reshape(-1, half_width), preferred_element_type=jnp.float32
        )
        full_sum = jnp.zeros((rack_rows, model_width), jnp.float32)
        full_sum = lax.dynamic_update_slice_in_dim(
            full_sum, partial_sum, half_index * half_width, 1
        )
        update = lax.psum_scatter(
            full_sum.astype(jnp.bfloat16), "expert", scatter_dimension=0, tiled=True
        ).astype(jnp.float32)
        residual = residual + update
    return residual


def solution(mesh):
    in_specs = (
        P(("rack", "expert"), None),
        P(),
        P(None, ("rack", "expert"), None),
        P(None, ("rack", "expert"), None),
        P("rack", "expert", None, None, None),
        P("rack", "expert", None, None),
    )
    out_specs = P(("rack", "expert"), None)
    dense = mesh.shape["rack"] <= TOP
    return jax.shard_map(
        dense_steps if dense else per_device, mesh=mesh, in_specs=in_specs, out_specs=out_specs, check_vma=False
    )
```

```python
import functools

import jax
import jax.numpy as jnp
from jax import lax
from jax.experimental import pallas as pl
from jax.experimental.pallas import tpu as pltpu
from jax.sharding import PartitionSpec as P

TOP = 8
STEPS = 4


def swapped(shard, axis, bit):
    return lax.ppermute(shard, axis, [(i, i ^ 1 << bit) for i in range(lax.axis_size(axis))])


def exchanged(shard, axis, mask):
    return lax.ppermute(shard, axis, [(i, i ^ mask) for i in range(lax.axis_size(axis))])


def widened(values):
    return values.astype(jnp.float32)


def rounded(values):
    return values.astype(jnp.bfloat16)


WHOLE = pl.BlockSpec(memory_space=pltpu.VMEM)
LANES = 128


def in_vmem(shape, dtype):
    return pltpu.VMEM(shape, dtype)


def kernel_call(body, out_shape, operands, flops):
    operands = [pltpu.with_memory_space_constraint(o, pltpu.VMEM) for o in operands]
    read = sum(o.size * o.dtype.itemsize for o in operands)
    return pl.pallas_call(
        body,
        out_shape=out_shape,
        in_specs=[WHOLE] * len(operands),
        out_specs=jax.tree.map(lambda _: WHOLE, out_shape),
        compiler_params=pltpu.CompilerParams(vmem_limit_bytes=24 * 2**20),
        cost_estimate=pl.CostEstimate(flops=flops, bytes_accessed=read, transcendentals=0),
    )(*operands)


def column_blocks(width):
    block = next(b for b in (512, 256, 128, width) if width % b == 0)
    return [slice(start, start + block) for start in range(0, width, block)]


def gate_up_body(has_update, *refs):
    if has_update:
        residual_ref, own_ref, other_ref, gain_ref, weight_ref, kept_ref, product_ref, message_ref = refs
        update = jnp.concatenate([own_ref[...], other_ref[...]], axis=0)
        residual = residual_ref[...] + widened(update)
        kept_ref[...] = residual
    else:
        residual_ref, gain_ref, weight_ref, product_ref, message_ref = refs
        residual = residual_ref[...]
    scaled = rounded(residual * gain_ref[...])
    width = weight_ref.shape[1]
    for columns in column_blocks(width):
        product = jnp.dot(scaled, weight_ref[:, columns], preferred_element_type=jnp.float32)
        product_ref[:, columns] = product
        message_ref[:, columns] = rounded(product)
    square_sum = jnp.sum(residual * residual, axis=1, keepdims=True)
    square_high = widened(rounded(square_sum))
    lane = lax.broadcasted_iota(jnp.int32, (residual.shape[0], LANES), 1)
    tail = jnp.where(lane == 0, square_high, square_sum - square_high)
    message_ref[:, width:] = rounded(tail)


def down_body(model_width, last, product_ref, message_ref, swapped_ref, weight_ref, mixing_ref, *out_refs):
    width = product_ref.shape[1]
    part = width // 2
    tails = widened(message_ref[:, width:]) + widened(swapped_ref[:, width:])
    square_sum = tails[:, 0:1] + tails[:, 1:2]
    scale = lax.rsqrt(square_sum / model_width + 1e-06)
    whole = product_ref[...] + widened(swapped_ref[:, :width])
    gate = whole[:, :part] * scale
    up = whole[:, part:] * scale
    activated = rounded(gate / (1.0 + jnp.exp(-gate)) * up)
    mixing = mixing_ref[...]
    half = mixing.shape[0] // 2
    for columns in column_blocks(weight_ref.shape[1]):
        term = jnp.dot(activated, weight_ref[:, columns], preferred_element_type=jnp.float32)
        update = widened(rounded(term)) * mixing
        if last:
            out_refs[0][:, columns] = rounded(update)
        else:
            out_refs[0][:, columns] = update[:half]
            out_refs[1][:, columns] = rounded(update[half:])


def dense_steps(hidden_in, norm_gain, expert_ids, gate_levels, w_gate_up, w_down):
    rack_count = lax.axis_size("rack")
    group_count = lax.axis_size("expert")
    rack_index = lax.axis_index("rack")
    group_index = lax.axis_index("expert")
    chip_count = rack_count // 2
    core_rows = chip_count * group_count
    token_count = 2 * core_rows
    model_width = hidden_in.shape[1]
    half_width = model_width // 2
    part_width = w_down.shape[2]
    first_half = group_index % 2 == 0
    gate_up_weight = w_gate_up[0, 0].reshape(half_width, 2 * part_width)
    down_weight = w_down[0, 0]

    def half_of(rows, own):
        return jnp.where(first_half == own, rows[:, :half_width], rows[:, half_width:])

    gain_half = half_of(norm_gain[None, :], True)

    routing = rounded(jnp.concatenate([expert_ids.reshape(1, -1), gate_levels.reshape(1, -1)], axis=1))
    route_width = STEPS * TOP
    message_width = -(-(half_width + 2 * route_width) // 2048) * 2048
    routing = jnp.pad(routing, ((0, 0), (0, message_width - half_width - 2 * route_width)))
    messages = jnp.concatenate([hidden_in.reshape(2, half_width), jnp.tile(routing, (2, 1))], axis=1)
    messages = messages.reshape(1, 2, message_width // 128, 128)
    messages = jnp.broadcast_to(messages, (token_count // 2,) + messages.shape[1:])
    messages = messages.reshape(token_count, message_width // 128, 128)
    messages = lax.all_to_all(messages, ("rack", "expert"), split_axis=0, concat_axis=0, tiled=True)
    messages = messages.reshape(token_count, message_width)
    token_ids = jnp.arange(token_count, dtype=jnp.int32)
    token_rack = token_ids // group_count
    place_of_token = (
        (token_rack % 2 ^ rack_index % 2) * core_rows
        + token_rack // 2 * group_count
        + token_ids % group_count
    )
    own_place = rack_index // 2 * group_count + group_index
    places = jnp.arange(token_count, dtype=jnp.int32)
    to_places = rounded(places[:, None] == place_of_token[None, :])
    rows = jnp.dot(to_places, messages, preferred_element_type=jnp.float32)
    residual = rows[:, :half_width]
    all_ids = rows[:, half_width : half_width + route_width].reshape(token_count, STEPS, TOP)
    all_levels = rows[:, half_width + route_width : half_width + 2 * route_width].reshape(
        token_count, STEPS, TOP
    )
    shares = all_levels / jnp.sum(all_levels, axis=-1, keepdims=True)
    mixing = jnp.sum(jnp.where(all_ids == rack_index.astype(jnp.float32), shares, 0.0), axis=2)
    mixing = widened(rounded(mixing))

    product_width = 2 * part_width
    product_flops = 2 * token_count * half_width * product_width
    sent = received = None
    for step_index in range(STEPS):
        last = step_index == STEPS - 1
        has_update = step_index > 0
        update_rows = [sent, received] if has_update else []
        kept = [in_vmem((token_count, half_width), jnp.float32)] if has_update else []
        *kept, product, message = kernel_call(
            functools.partial(gate_up_body, has_update),
            kept
            + [
                in_vmem((token_count, product_width), jnp.float32),
                in_vmem((token_count, product_width + LANES), jnp.bfloat16),
            ],
            [residual] + update_rows + [gain_half, gate_up_weight],
            product_flops,
        )
        if has_update:
            residual = kept[0]
        swapped_rows = exchanged(message, "expert", 1)
        if last:
            out_shape = [in_vmem((token_count, half_width), jnp.bfloat16)]
        else:
            out_shape = [
                in_vmem((core_rows, half_width), jnp.float32),
                in_vmem((core_rows, half_width), jnp.bfloat16),
            ]
        outs = kernel_call(
            functools.partial(down_body, model_width, last),
            out_shape,
            [product, message, swapped_rows, down_weight, mixing[:, step_index : step_index + 1]],
            product_flops // 2,
        )
        if last:
            update = outs[0]
            break
        update = outs[0] + widened(exchanged(outs[1], "rack", 1))
        sent = rounded(update)
        update = widened(sent)
        for mask in range(2, rack_count, 2):
            update = update + widened(exchanged(sent, "rack", mask))
        sent = rounded(update)
        update = widened(sent)
        for mask in range(2, group_count, 2):
            update = update + widened(exchanged(sent, "expert", mask))
        sent = rounded(update)
        received = exchanged(sent, "rack", 1)

    to_tokens = rounded(place_of_token[:, None] == places[None, :])
    outgoing = rounded(
        jnp.dot(to_tokens, update, preferred_element_type=jnp.float32)
    )
    arrived = lax.all_to_all(
        outgoing.reshape(token_count, half_width // 128, 128),
        ("rack", "expert"), split_axis=0, concat_axis=0, tiled=True,
    ).reshape(token_count, half_width)
    arrived = widened(arrived)
    is_first = token_ids[:, None] % 2 == 0
    update = jnp.concatenate(
        [
            jnp.sum(jnp.where(is_first, arrived, 0.0), axis=0, keepdims=True),
            jnp.sum(jnp.where(is_first, 0.0, arrived), axis=0, keepdims=True),
        ],
        axis=1,
    )
    own_row = jnp.sum(jnp.where(places[:, None] == own_place, residual, 0.0), axis=0, keepdims=True)
    other_row = jnp.sum(
        jnp.where(places[:, None] == (own_place ^ 1), residual, 0.0), axis=0, keepdims=True
    )
    other_row = exchanged(other_row, "expert", 1)
    own_residual = jnp.where(
        first_half,
        jnp.concatenate([own_row, other_row], axis=1),
        jnp.concatenate([other_row, own_row], axis=1),
    )
    return own_residual + update


def per_device(hidden_in, norm_gain, expert_ids, gate_levels, w_gate_up, w_down):
    rack_count = lax.axis_size("rack")
    group_count = lax.axis_size("expert")
    group_index = lax.axis_index("expert")
    half_index = group_index % 2
    tok_rows = hidden_in.shape[0]
    rack_rows = tok_rows * group_count
    slot_count = min(rack_rows, 3 * rack_rows * TOP // (2 * rack_count))
    model_width = hidden_in.shape[1]
    half_width = model_width // 2
    part_width = w_down.shape[2]
    gate_up_weight = w_gate_up[0, 0].reshape(half_width, 2 * part_width)
    down_weight = w_down[0, 0]
    all_ids, all_levels = (
        lax.all_gather(expert_ids, "expert", axis=1, tiled=True),
        lax.all_gather(gate_levels, "expert", axis=1, tiled=True),
    )
    expert_range = jnp.arange(rack_count, dtype=jnp.int32)
    slot_ids = jnp.arange(slot_count, dtype=jnp.int32)
    residual = hidden_in.astype(jnp.float32)
    for step_index in range(STEPS):
        mean_square = jnp.mean(residual * residual, axis=-1, keepdims=True)
        normed = (residual * lax.rsqrt(mean_square + 1e-06) * norm_gain).astype(jnp.bfloat16)
        rack_normed = lax.all_gather(normed, "expert", axis=0, tiled=True)
        picked = all_ids[step_index]
        level_vals = all_levels[step_index].astype(jnp.float32)
        shares = level_vals / jnp.sum(level_vals, axis=-1, keepdims=True)
        matches = picked[:, :, None] == expert_range[None, None, :]
        chosen = jnp.sum(matches.astype(jnp.int32), axis=1)
        mixing = jnp.sum(jnp.where(matches, shares[:, :, None], jnp.float32(0.0)), axis=1).astype(
            jnp.bfloat16
        )
        slot_rank = jnp.cumsum(chosen, axis=0) - chosen
        placement = chosen[:, :, None] * (slot_rank[:, :, None] == slot_ids).astype(jnp.int32)
        dispatch_map = (
            jnp.transpose(placement, (1, 2, 0))
            .reshape(rack_count * slot_count, rack_rows)
            .astype(jnp.bfloat16)
        )
        outgoing = jnp.dot(dispatch_map, rack_normed, preferred_element_type=jnp.float32).astype(
            jnp.bfloat16
        )
        outgoing = outgoing.reshape(rack_count, slot_count, model_width)
        combine_map = (placement.astype(jnp.bfloat16) * mixing[:, :, None]).reshape(
            rack_rows, rack_count * slot_count
        )
        half_rows = lax.dynamic_slice_in_dim(outgoing, half_index * half_width, half_width, 2)
        slot_rows = lax.all_to_all(half_rows, "rack", split_axis=0, concat_axis=0, tiled=True)
        layout = slot_rows.shape
        flat_rows = slot_rows.reshape(-1, half_width)
        gate_up = jnp.dot(flat_rows, gate_up_weight, preferred_element_type=jnp.float32)
        gate_up = gate_up + swapped(gate_up.astype(jnp.bfloat16), "expert", 0).astype(gate_up.dtype)
        activated = (jax.nn.silu(gate_up[:, :part_width]) * gate_up[:, part_width:]).astype(
            jnp.bfloat16
        )
        partial_value = jnp.dot(activated, down_weight, preferred_element_type=jnp.float32).astype(
            jnp.bfloat16
        )
        partial_value = partial_value.reshape(layout)
        finished = lax.all_to_all(partial_value, "rack", split_axis=0, concat_axis=0, tiled=True)
        partial_sum = jnp.dot(
            combine_map, finished.reshape(-1, half_width), preferred_element_type=jnp.float32
        )
        full_sum = jnp.zeros((rack_rows, model_width), jnp.float32)
        full_sum = lax.dynamic_update_slice_in_dim(
            full_sum, partial_sum, half_index * half_width, 1
        )
        update = lax.psum_scatter(
            full_sum.astype(jnp.bfloat16), "expert", scatter_dimension=0, tiled=True
        ).astype(jnp.float32)
        residual = residual + update
    return residual


def solution(mesh):
    in_specs = (
        P(("rack", "expert"), None),
        P(),
        P(None, ("rack", "expert"), None),
        P(None, ("rack", "expert"), None),
        P("rack", "expert", None, None, None),
        P("rack", "expert", None, None),
    )
    out_specs = P(("rack", "expert"), None)
    dense = mesh.shape["rack"] <= TOP
    return jax.shard_map(
        dense_steps if dense else per_device, mesh=mesh, in_specs=in_specs, out_specs=out_specs, check_vma=False
    )
```

```python
import functools

import jax
import jax.numpy as jnp
from jax import lax
from jax.experimental import pallas as pl
from jax.experimental.pallas import tpu as pltpu
from jax.sharding import PartitionSpec as P

TOP = 8
STEPS = 4


def swapped(shard, axis, bit):
    return lax.ppermute(shard, axis, [(i, i ^ 1 << bit) for i in range(lax.axis_size(axis))])


def exchanged(shard, axis, mask):
    return lax.ppermute(shard, axis, [(i, i ^ mask) for i in range(lax.axis_size(axis))])


def widened(values):
    return values.astype(jnp.float32)


def rounded(values):
    return values.astype(jnp.bfloat16)


WHOLE = pl.BlockSpec(memory_space=pltpu.VMEM)
IN_HBM = pl.BlockSpec(memory_space=pltpu.HBM)
LANES = 128


def in_vmem(shape, dtype):
    return pltpu.VMEM(shape, dtype)


def kernel_call(body, out_shape, operands, flops=0, in_hbm=(), scratch=(), limit=4):
    operands = [pltpu.with_memory_space_constraint(o, pltpu.VMEM) for o in operands]
    in_hbm = [pltpu.with_memory_space_constraint(o, pltpu.HBM) for o in in_hbm]
    read = sum(o.size * o.dtype.itemsize for o in [*operands, *in_hbm])
    return pl.pallas_call(
        body,
        out_shape=out_shape,
        in_specs=[WHOLE] * len(operands) + [IN_HBM] * len(in_hbm),
        out_specs=[WHOLE] * len(out_shape),
        scratch_shapes=scratch,
        compiler_params=pltpu.CompilerParams(vmem_limit_bytes=limit * 2**20),
        cost_estimate=pl.CostEstimate(flops=flops, bytes_accessed=read, transcendentals=0),
    )(*operands, *in_hbm)


def column_blocks(width):
    block = next(b for b in (512, 256, 128, width) if width % b == 0)
    return [slice(start, start + block) for start in range(0, width, block)]


def row_blocks(values, start, stop):
    return [values[:, at : at + LANES] for at in range(start, stop, LANES)]


def message_body(hidden_in, ids_in, levels_in, gain_in, own_ref, other_ref, gain_ref, hidden, ids, levels, gain, semaphores):
    copies = [
        pltpu.make_async_copy(source, target, semaphores.at[k])
        for k, (source, target) in enumerate(
            [(hidden_in, hidden), (ids_in, ids), (levels_in, levels), (gain_in, gain)]
        )
    ]
    for copy in copies:
        copy.start()
    for copy in copies:
        copy.wait()
    half_width = hidden.shape[1] // 2
    half_rows = half_width // LANES
    is_first = lax.axis_index("expert") % 2 == 0
    row = lax.broadcasted_iota(jnp.int32, own_ref.shape, 0)

    def route_row(ref):
        values = [widened(ref[step]) for step in range(ref.shape[0])]
        used = len(values) * values[0].shape[1]
        return jnp.concatenate(values + [jnp.zeros((1, LANES - used), jnp.float32)], axis=1)

    routing = [route_row(ids), route_row(levels)]
    features = widened(hidden[...])
    first = row_blocks(features, 0, half_width)
    second = row_blocks(features, half_width, 2 * half_width)
    for target, pairs in ((own_ref, zip(first, second)), (other_ref, zip(second, first))):
        message = jnp.zeros(own_ref.shape, jnp.float32)
        for place, values in enumerate([jnp.where(is_first, a, b) for a, b in pairs] + routing):
            message = jnp.where(row == place, values, message)
        target[...] = rounded(message)
    for place in range(half_rows):
        gain_ref[:, place * LANES : (place + 1) * LANES] = jnp.where(
            is_first, gain[place : place + 1], gain[half_rows + place : half_rows + place + 1]
        )


def weights_body(gate_up_ref, weight_ref, arrived_ref, semaphores):
    part = arrived_ref.shape[2]
    count = semaphores.shape[0]
    block = arrived_ref.shape[0] // count
    blocks = [pl.ds(k * block, block) for k in range(count)]
    copies = [
        pltpu.make_async_copy(gate_up_ref.at[rows], arrived_ref.at[rows], semaphores.at[k])
        for k, rows in enumerate(blocks)
    ]
    for copy in copies:
        copy.start()
    for copy, rows in zip(copies, blocks):
        copy.wait()
        weight_ref[rows] = arrived_ref[rows].reshape(block, 2 * part)


def joined_body(ready_ref, *refs):
    *pieces, out_ref = refs
    size = out_ref.shape[0] // len(pieces)
    for k, piece in enumerate(pieces):
        out_ref[k * size : (k + 1) * size] = piece[...].reshape(size, *out_ref.shape[1:])


def own_place_of(group_count):
    return lax.axis_index("rack") // 2 * group_count + lax.axis_index("expert")


def placed(gathered_refs, half_width, group_count):
    wide = jnp.concatenate([ref[...].reshape(ref.shape[0], -1) for ref in gathered_refs], axis=0)
    count = wide.shape[0]
    place = lax.broadcasted_iota(jnp.int32, (count, count), 0)
    source = lax.broadcasted_iota(jnp.int32, (count, count), 1)
    to_place = rounded(jnp.where(place == (source ^ own_place_of(group_count)), 1.0, 0.0))
    wide = jnp.dot(to_place, wide, preferred_element_type=jnp.float32)
    residual = wide[:, :half_width]
    ids = wide[:, half_width : half_width + LANES]
    levels = wide[:, half_width + LANES : half_width + 2 * LANES]
    lane = lax.broadcasted_iota(jnp.int32, ids.shape, 1)
    chosen = ids == lax.axis_index("rack").astype(jnp.float32)
    mixing = jnp.zeros(ids.shape, jnp.float32)
    for step in range(STEPS):
        of_step = lane // TOP == step
        total = jnp.sum(jnp.where(of_step, levels, 0.0), axis=1, keepdims=True)
        share = jnp.sum(jnp.where(of_step & chosen, levels / total, 0.0), axis=1, keepdims=True)
        mixing = jnp.where(lane == step, widened(rounded(share)), mixing)
    return residual, mixing


def gate_up_body(step, group_count, *refs):
    first, last = step == 0, step == STEPS - 1
    if first:
        *gathered_refs, gain_ref, weight_ref, residual_ref, mixing_ref, product_ref, message_ref = refs
        residual, mixing_ref[...] = placed(gathered_refs, gain_ref.shape[1], group_count)
        residual_ref[...] = residual
    else:
        before_ref, own_ref, other_ref, gain_ref, weight_ref, *residual_refs, product_ref, message_ref = refs
        update = jnp.concatenate([own_ref[...], other_ref[...]], axis=0)
        residual = before_ref[...] + widened(update)
        if last:
            place = lax.broadcasted_iota(jnp.int32, (residual.shape[0], 1), 0)
            own_place = own_place_of(group_count)
            for ref, wanted in zip(residual_refs, (own_place, own_place ^ 1)):
                ref[...] = jnp.sum(jnp.where(place == wanted, residual, 0.0), axis=0, keepdims=True)
        else:
            residual_refs[0][...] = residual
    scaled = rounded(residual * gain_ref[...])
    width = weight_ref.shape[1]
    for columns in column_blocks(width):
        product = jnp.dot(scaled, weight_ref[:, columns], preferred_element_type=jnp.float32)
        product_ref[:, columns] = product
        message_ref[:, columns] = rounded(product)
    square_sum = jnp.sum(residual * residual, axis=1, keepdims=True)
    square_high = widened(rounded(square_sum))
    lane = lax.broadcasted_iota(jnp.int32, (residual.shape[0], LANES), 1)
    tail = jnp.where(lane == 0, square_high, square_sum - square_high)
    message_ref[:, width:] = rounded(tail)


def token_matrix(count, group_count):
    token = lax.broadcasted_iota(jnp.int32, (count, count), 0)
    place = lax.broadcasted_iota(jnp.int32, (count, count), 1)
    rack = token // group_count
    core = (rack + lax.axis_index("rack")) % 2
    matches = core * (count // 2) + rack // 2 * group_count + token % group_count == place
    return rounded(jnp.where(matches, 1.0, 0.0))


def down_body(step, model_width, group_count, product_ref, message_ref, swapped_ref, mixing_ref, weight_ref, *out_refs):
    width = product_ref.shape[1]
    part = width // 2
    tails = widened(message_ref[:, width:]) + widened(swapped_ref[:, width:])
    square_sum = tails[:, 0:1] + tails[:, 1:2]
    scale = lax.rsqrt(square_sum / model_width + 1e-06)
    whole = product_ref[...] + widened(swapped_ref[:, :width])
    gate = whole[:, :part] * scale
    up = whole[:, part:] * scale
    activated = rounded(gate / (1.0 + jnp.exp(-gate)) * up)
    mixing = mixing_ref[...]
    count = mixing.shape[0]
    last = step == STEPS - 1
    if last:
        to_tokens = token_matrix(count, group_count)
        activated = rounded(jnp.dot(to_tokens, activated, preferred_element_type=jnp.float32))
        mixing = jnp.dot(to_tokens, rounded(mixing), preferred_element_type=jnp.float32)
    mixing = mixing[:, step : step + 1]
    for columns in column_blocks(weight_ref.shape[1]):
        term = jnp.dot(activated, weight_ref[:, columns], preferred_element_type=jnp.float32)
        update = widened(rounded(term)) * mixing
        if last:
            blocks = slice(columns.start // LANES, columns.stop // LANES)
            out_refs[0][:, blocks] = rounded(update).reshape(count, -1, LANES)
        else:
            out_refs[0][:, columns] = update[: count // 2]
            out_refs[1][:, columns] = rounded(update[count // 2 :])


def result_body(arrived_ref, own_ref, other_ref, out_ref):
    count, half_width = arrived_ref.shape[0], own_ref.shape[1]
    terms = widened(arrived_ref[...].reshape(count, half_width))
    of_first = lax.broadcasted_iota(jnp.int32, (count, 1), 0) % 2 == 0
    is_first = lax.axis_index("expert") % 2 == 0
    own, other = own_ref[...], other_ref[...]
    out_ref[:, :half_width] = jnp.where(is_first, own, other) + jnp.sum(
        jnp.where(of_first, terms, 0.0), axis=0, keepdims=True
    )
    out_ref[:, half_width:] = jnp.where(is_first, other, own) + jnp.sum(
        jnp.where(of_first, 0.0, terms), axis=0, keepdims=True
    )


def dense_steps(hidden_in, norm_gain, expert_ids, gate_levels, w_gate_up, w_down):
    rack_count = lax.axis_size("rack")
    group_count = lax.axis_size("expert")
    core_rows = rack_count // 2 * group_count
    token_count = 2 * core_rows
    model_width = hidden_in.shape[1]
    half_width = model_width // 2
    part_width = w_down.shape[2]
    product_width = 2 * part_width
    product_flops = 2 * token_count * half_width * product_width

    block_shape = (half_width // LANES + 2, LANES)
    sources = [hidden_in, expert_ids, gate_levels, norm_gain.reshape(-1, LANES)]
    own, other, gain_half = kernel_call(
        message_body,
        [
            in_vmem(block_shape, jnp.bfloat16),
            in_vmem(block_shape, jnp.bfloat16),
            in_vmem((1, half_width), jnp.float32),
        ],
        [],
        in_hbm=sources,
        scratch=[*(in_vmem(a.shape, a.dtype) for a in sources), pltpu.SemaphoreType.DMA((len(sources),))],
    )
    block = next(b for b in (128, 16, half_width) if half_width % b == 0)
    (gate_up_weight,) = kernel_call(
        weights_body,
        [in_vmem((half_width, product_width), jnp.bfloat16)],
        [],
        in_hbm=[w_gate_up[0, 0]],
        scratch=[
            in_vmem((half_width, 2, part_width), jnp.bfloat16),
            pltpu.SemaphoreType.DMA((half_width // block,)),
        ],
        limit=12,
    )

    def joined(ready, pieces, count):
        out_shape = [in_vmem((count,) + block_shape, jnp.bfloat16)]
        return kernel_call(joined_body, out_shape, [ready, *pieces])[0]

    rows = [own] + [exchanged(other if mask % 2 else own, "expert", mask) for mask in range(1, group_count)]
    rows = joined(gate_up_weight, rows, group_count)
    rows = [rows] + [exchanged(rows, "rack", mask) for mask in range(2, rack_count, 2)]
    rows = joined(gate_up_weight, rows, core_rows)
    gathered = [rows, exchanged(rows, "rack", 1)]

    for step_index in range(STEPS):
        last = step_index == STEPS - 1
        products = [
            in_vmem((token_count, product_width), jnp.float32),
            in_vmem((token_count, product_width + LANES), jnp.bfloat16),
        ]
        kept = [in_vmem((token_count, half_width), jnp.float32)]
        if step_index == 0:
            operands = gathered
            kept += [in_vmem((token_count, LANES), jnp.float32)]
        else:
            operands = [residual, sent, received]
        if last:
            kept = [in_vmem((1, half_width), jnp.float32)] * 2
        *kept, product, message = kernel_call(
            functools.partial(gate_up_body, step_index, group_count),
            kept + products,
            operands + [gain_half, gate_up_weight],
            product_flops,
        )
        if step_index == 0:
            residual, mixing = kept
        else:
            residual = kept[0]
        swapped_rows = exchanged(message, "expert", 1)
        if last:
            own_row, other_row = kept
            other_row = exchanged(other_row, "expert", 1)
            swapped_rows, other_row = lax.optimization_barrier((swapped_rows, other_row))
            updates = [in_vmem((token_count, half_width // LANES, LANES), jnp.bfloat16)]
        else:
            updates = [
                in_vmem((core_rows, half_width), jnp.float32),
                in_vmem((core_rows, half_width), jnp.bfloat16),
            ]
        updates = kernel_call(
            functools.partial(down_body, step_index, model_width, group_count),
            updates,
            [product, message, swapped_rows, mixing, w_down[0, 0]],
            product_flops // 2,
        )
        if last:
            break
        update = updates[0] + widened(exchanged(updates[1], "rack", 1))
        sent = rounded(update)
        update = widened(sent)
        for mask in range(2, rack_count, 2):
            update = update + widened(exchanged(sent, "rack", mask))
        sent = rounded(update)
        update = widened(sent)
        for mask in range(2, group_count, 2):
            update = update + widened(exchanged(sent, "expert", mask))
        sent = rounded(update)
        received = exchanged(sent, "rack", 1)

    arrived = lax.all_to_all(updates[0], ("rack", "expert"), split_axis=0, concat_axis=0, tiled=True)
    (result,) = kernel_call(
        result_body, [jax.ShapeDtypeStruct((1, model_width), jnp.float32)], [arrived, own_row, other_row]
    )
    return result


def per_device(hidden_in, norm_gain, expert_ids, gate_levels, w_gate_up, w_down):
    rack_count = lax.axis_size("rack")
    group_count = lax.axis_size("expert")
    group_index = lax.axis_index("expert")
    half_index = group_index % 2
    tok_rows = hidden_in.shape[0]
    rack_rows = tok_rows * group_count
    slot_count = min(rack_rows, 3 * rack_rows * TOP // (2 * rack_count))
    model_width = hidden_in.shape[1]
    half_width = model_width // 2
    part_width = w_down.shape[2]
    gate_up_weight = w_gate_up[0, 0].reshape(half_width, 2 * part_width)
    down_weight = w_down[0, 0]
    all_ids, all_levels = (
        lax.all_gather(expert_ids, "expert", axis=1, tiled=True),
        lax.all_gather(gate_levels, "expert", axis=1, tiled=True),
    )
    expert_range = jnp.arange(rack_count, dtype=jnp.int32)
    slot_ids = jnp.arange(slot_count, dtype=jnp.int32)
    residual = hidden_in.astype(jnp.float32)
    for step_index in range(STEPS):
        mean_square = jnp.mean(residual * residual, axis=-1, keepdims=True)
        normed = (residual * lax.rsqrt(mean_square + 1e-06) * norm_gain).astype(jnp.bfloat16)
        rack_normed = lax.all_gather(normed, "expert", axis=0, tiled=True)
        picked = all_ids[step_index]
        level_vals = all_levels[step_index].astype(jnp.float32)
        shares = level_vals / jnp.sum(level_vals, axis=-1, keepdims=True)
        matches = picked[:, :, None] == expert_range[None, None, :]
        chosen = jnp.sum(matches.astype(jnp.int32), axis=1)
        mixing = jnp.sum(jnp.where(matches, shares[:, :, None], jnp.float32(0.0)), axis=1).astype(
            jnp.bfloat16
        )
        slot_rank = jnp.cumsum(chosen, axis=0) - chosen
        placement = chosen[:, :, None] * (slot_rank[:, :, None] == slot_ids).astype(jnp.int32)
        dispatch_map = (
            jnp.transpose(placement, (1, 2, 0))
            .reshape(rack_count * slot_count, rack_rows)
            .astype(jnp.bfloat16)
        )
        outgoing = jnp.dot(dispatch_map, rack_normed, preferred_element_type=jnp.float32).astype(
            jnp.bfloat16
        )
        outgoing = outgoing.reshape(rack_count, slot_count, model_width)
        combine_map = (placement.astype(jnp.bfloat16) * mixing[:, :, None]).reshape(
            rack_rows, rack_count * slot_count
        )
        half_rows = lax.dynamic_slice_in_dim(outgoing, half_index * half_width, half_width, 2)
        slot_rows = lax.all_to_all(half_rows, "rack", split_axis=0, concat_axis=0, tiled=True)
        layout = slot_rows.shape
        flat_rows = slot_rows.reshape(-1, half_width)
        gate_up = jnp.dot(flat_rows, gate_up_weight, preferred_element_type=jnp.float32)
        gate_up = gate_up + swapped(gate_up.astype(jnp.bfloat16), "expert", 0).astype(gate_up.dtype)
        activated = (jax.nn.silu(gate_up[:, :part_width]) * gate_up[:, part_width:]).astype(
            jnp.bfloat16
        )
        partial_value = jnp.dot(activated, down_weight, preferred_element_type=jnp.float32).astype(
            jnp.bfloat16
        )
        partial_value = partial_value.reshape(layout)
        finished = lax.all_to_all(partial_value, "rack", split_axis=0, concat_axis=0, tiled=True)
        partial_sum = jnp.dot(
            combine_map, finished.reshape(-1, half_width), preferred_element_type=jnp.float32
        )
        full_sum = jnp.zeros((rack_rows, model_width), jnp.float32)
        full_sum = lax.dynamic_update_slice_in_dim(
            full_sum, partial_sum, half_index * half_width, 1
        )
        update = lax.psum_scatter(
            full_sum.astype(jnp.bfloat16), "expert", scatter_dimension=0, tiled=True
        ).astype(jnp.float32)
        residual = residual + update
    return residual


def solution(mesh):
    in_specs = (
        P(("rack", "expert"), None),
        P(),
        P(None, ("rack", "expert"), None),
        P(None, ("rack", "expert"), None),
        P("rack", "expert", None, None, None),
        P("rack", "expert", None, None),
    )
    out_specs = P(("rack", "expert"), None)
    dense = mesh.shape["rack"] <= TOP
    return jax.shard_map(
        dense_steps if dense else per_device, mesh=mesh, in_specs=in_specs, out_specs=out_specs, check_vma=False
    )
```

```python
import functools

import jax
import jax.numpy as jnp
from jax import lax
from jax.experimental import pallas as pl
from jax.experimental.pallas import tpu as pltpu
from jax.sharding import PartitionSpec as P

TOP = 8
STEPS = 4


def swapped(shard, axis, bit):
    return lax.ppermute(shard, axis, [(i, i ^ 1 << bit) for i in range(lax.axis_size(axis))])


def exchanged(shard, axis, mask):
    return lax.ppermute(shard, axis, [(i, i ^ mask) for i in range(lax.axis_size(axis))])


def widened(values):
    return values.astype(jnp.float32)


def rounded(values):
    return values.astype(jnp.bfloat16)


def exchanged_both(shard, rack_mask, expert_mask):
    groups = lax.axis_size("expert")
    pairs = [
        (rack * groups + group, (rack ^ rack_mask) * groups + (group ^ expert_mask))
        for rack in range(lax.axis_size("rack"))
        for group in range(groups)
    ]
    return lax.ppermute(shard, ("rack", "expert"), pairs)


def gather_masks(rack_count, group_count):
    near = [(rack, group) for group in (0, 1) for rack in (0, 2)]
    far = [(rack, group) for group in range(0, group_count, 2) for rack in range(0, rack_count, 4)]
    return near, far


WHOLE = pl.BlockSpec(memory_space=pltpu.VMEM)
IN_HBM = pl.BlockSpec(memory_space=pltpu.HBM)
LANES = 128
PIECES = 2


def in_vmem(shape, dtype):
    return pltpu.VMEM(shape, dtype)


def kernel_call(body, out_shape, operands, flops=0, in_hbm=(), scratch=(), limit=4):
    operands = [pltpu.with_memory_space_constraint(o, pltpu.VMEM) for o in operands]
    in_hbm = [pltpu.with_memory_space_constraint(o, pltpu.HBM) for o in in_hbm]
    read = sum(o.size * o.dtype.itemsize for o in [*operands, *in_hbm])
    return pl.pallas_call(
        body,
        out_shape=out_shape,
        in_specs=[WHOLE] * len(operands) + [IN_HBM] * len(in_hbm),
        out_specs=[WHOLE] * len(out_shape),
        scratch_shapes=scratch,
        compiler_params=pltpu.CompilerParams(vmem_limit_bytes=limit * 2**20),
        cost_estimate=pl.CostEstimate(flops=flops, bytes_accessed=read, transcendentals=0),
    )(*operands, *in_hbm)


def column_blocks(width):
    block = next(b for b in (512, 256, 128, width) if width % b == 0)
    return [slice(start, start + block) for start in range(0, width, block)]


def row_blocks(values, start, stop):
    return [values[:, at : at + LANES] for at in range(start, stop, LANES)]


def message_body(hidden_in, ids_in, levels_in, gain_in, own_ref, other_ref, gain_ref, hidden, ids, levels, gain, semaphores):
    copies = [
        pltpu.make_async_copy(source, target, semaphores.at[k])
        for k, (source, target) in enumerate(
            [(hidden_in, hidden), (ids_in, ids), (levels_in, levels), (gain_in, gain)]
        )
    ]
    for copy in copies:
        copy.start()
    for copy in copies:
        copy.wait()
    half_width = hidden.shape[1] // 2
    half_rows = half_width // LANES
    is_first = lax.axis_index("expert") % 2 == 0
    row = lax.broadcasted_iota(jnp.int32, own_ref.shape, 0)

    def route_row(ref):
        values = [widened(ref[step]) for step in range(ref.shape[0])]
        used = len(values) * values[0].shape[1]
        return jnp.concatenate(values + [jnp.zeros((1, LANES - used), jnp.float32)], axis=1)

    routing = [route_row(ids), route_row(levels)]
    features = widened(hidden[...])
    first = row_blocks(features, 0, half_width)
    second = row_blocks(features, half_width, 2 * half_width)
    for target, pairs in ((own_ref, zip(first, second)), (other_ref, zip(second, first))):
        message = jnp.zeros(own_ref.shape, jnp.float32)
        for place, values in enumerate([jnp.where(is_first, a, b) for a, b in pairs] + routing):
            message = jnp.where(row == place, values, message)
        target[...] = rounded(message)
    for place in range(half_rows):
        gain_ref[:, place * LANES : (place + 1) * LANES] = jnp.where(
            is_first, gain[place : place + 1], gain[half_rows + place : half_rows + place + 1]
        )


def weights_body(gate_up_ref, weight_ref, arrived_ref, semaphores):
    part = arrived_ref.shape[2]
    count = semaphores.shape[0]
    block = arrived_ref.shape[0] // count
    blocks = [pl.ds(k * block, block) for k in range(count)]
    copies = [
        pltpu.make_async_copy(gate_up_ref.at[rows], arrived_ref.at[rows], semaphores.at[k])
        for k, rows in enumerate(blocks)
    ]
    for copy in copies:
        copy.start()
    for copy, rows in zip(copies, blocks):
        copy.wait()
        weight_ref[rows] = arrived_ref[rows].reshape(block, 2 * part)


def joined_body(ready_ref, *refs):
    *pieces, out_ref = refs
    size = out_ref.shape[0] // len(pieces)
    for k, piece in enumerate(pieces):
        out_ref[k * size : (k + 1) * size] = piece[...].reshape(size, *out_ref.shape[1:])


def own_place_of(group_count):
    return lax.axis_index("rack") // 2 * group_count + lax.axis_index("expert")


def placed(gathered_refs, half_width, rack_count, group_count):
    wide = jnp.concatenate([ref[...].reshape(ref.shape[0], -1) for ref in gathered_refs], axis=0)
    count = wide.shape[0]
    place = lax.broadcasted_iota(jnp.int32, (count, count), 0)
    source = lax.broadcasted_iota(jnp.int32, (count, count), 1)
    near, far = gather_masks(rack_count, group_count)
    distance = source // (count // 2) * (count // 2)
    for masks, index in ((near, source % len(near)), (far, source // len(near) % len(far))):
        for k, (rack, group) in enumerate(masks):
            distance = distance + jnp.where(index == k, rack // 2 * group_count + group, 0)
    to_place = rounded(jnp.where(place == (distance ^ own_place_of(group_count)), 1.0, 0.0))
    wide = jnp.dot(to_place, wide, preferred_element_type=jnp.float32)
    residual = wide[:, :half_width]
    ids = wide[:, half_width : half_width + LANES]
    levels = wide[:, half_width + LANES : half_width + 2 * LANES]
    lane = lax.broadcasted_iota(jnp.int32, ids.shape, 1)
    chosen = ids == lax.axis_index("rack").astype(jnp.float32)
    mixing = jnp.zeros(ids.shape, jnp.float32)
    for step in range(STEPS):
        of_step = lane // TOP == step
        total = jnp.sum(jnp.where(of_step, levels, 0.0), axis=1, keepdims=True)
        share = jnp.sum(jnp.where(of_step & chosen, levels / total, 0.0), axis=1, keepdims=True)
        mixing = jnp.where(lane == step, widened(rounded(share)), mixing)
    return residual, mixing


def piece_columns(piece, part):
    size = part // PIECES
    return [slice(start, start + size) for start in (piece * size, part + piece * size)]


def multiplied(scaled, weight_ref, piece, product_ref, message_ref):
    size = weight_ref.shape[1] // 2 // PIECES
    for k, columns in enumerate(piece_columns(piece, weight_ref.shape[1] // 2)):
        product = jnp.dot(scaled, weight_ref[:, columns], preferred_element_type=jnp.float32)
        product_ref[:, k * size : (k + 1) * size] = product
        message_ref[:, k * size : (k + 1) * size] = rounded(product)


def first_piece_body(step, rack_count, group_count, *refs):
    first, last = step == 0, step == STEPS - 1
    if first:
        *gathered_refs, gain_ref, weight_ref, residual_ref, mixing_ref, scaled_ref, product_ref, message_ref = refs
        residual, mixing_ref[...] = placed(gathered_refs, gain_ref.shape[1], rack_count, group_count)
        residual_ref[...] = residual
    else:
        before_ref, own_ref, other_ref, gain_ref, weight_ref, *residual_refs, scaled_ref, product_ref, message_ref = refs
        update = jnp.concatenate([own_ref[...], other_ref[...]], axis=0)
        residual = before_ref[...] + widened(update)
        if last:
            place = lax.broadcasted_iota(jnp.int32, (residual.shape[0], 1), 0)
            own_place = own_place_of(group_count)
            for ref, wanted in zip(residual_refs, (own_place, own_place ^ 1)):
                ref[...] = jnp.sum(jnp.where(place == wanted, residual, 0.0), axis=0, keepdims=True)
        else:
            residual_refs[0][...] = residual
    scaled = rounded(residual * gain_ref[...])
    scaled_ref[...] = scaled
    multiplied(scaled, weight_ref, 0, product_ref, message_ref)
    square_sum = jnp.sum(residual * residual, axis=1, keepdims=True)
    square_high = widened(rounded(square_sum))
    lane = lax.broadcasted_iota(jnp.int32, (residual.shape[0], LANES), 1)
    tail = jnp.where(lane == 0, square_high, square_sum - square_high)
    message_ref[:, product_ref.shape[1] :] = rounded(tail)


def other_piece_body(piece, scaled_ref, weight_ref, product_ref, message_ref):
    multiplied(scaled_ref[...], weight_ref, piece, product_ref, message_ref)


def token_matrix(count, group_count):
    token = lax.broadcasted_iota(jnp.int32, (count, count), 0)
    place = lax.broadcasted_iota(jnp.int32, (count, count), 1)
    rack = token // group_count
    core = (rack + lax.axis_index("rack")) % 2
    matches = core * (count // 2) + rack // 2 * group_count + token % group_count == place
    return rounded(jnp.where(matches, 1.0, 0.0))


def down_body(step, piece, model_width, group_count, tail_ref, other_tail_ref, product_ref, swapped_ref, mixing_ref, weight_ref, *refs):
    width = product_ref.shape[1]
    size = width // 2
    tails = widened(tail_ref[:, width:]) + widened(other_tail_ref[:, width:])
    square_sum = tails[:, 0:1] + tails[:, 1:2]
    scale = lax.rsqrt(square_sum / model_width + 1e-06)
    whole = product_ref[...] + widened(swapped_ref[:, :width])
    gate = whole[:, :size] * scale
    up = whole[:, size:] * scale
    activated = rounded(gate / (1.0 + jnp.exp(-gate)) * up)
    mixing = mixing_ref[...]
    count = mixing.shape[0]
    last = step == STEPS - 1
    if last:
        to_tokens = token_matrix(count, group_count)
        activated = rounded(jnp.dot(to_tokens, activated, preferred_element_type=jnp.float32))
        mixing = jnp.dot(to_tokens, rounded(mixing), preferred_element_type=jnp.float32)
    mixing = mixing[:, step : step + 1]
    rows = slice(piece * size, (piece + 1) * size)
    before_refs, out_refs = (refs[:1], refs[1:]) if piece else ((), refs)
    for columns in column_blocks(weight_ref.shape[1]):
        term = jnp.dot(activated, weight_ref[rows, columns], preferred_element_type=jnp.float32)
        for ref in before_refs:
            term = term + ref[:, columns]
        if piece < PIECES - 1:
            out_refs[0][:, columns] = term
            continue
        update = widened(rounded(term)) * mixing
        if last:
            blocks = slice(columns.start // LANES, columns.stop // LANES)
            out_refs[0][:, blocks] = rounded(update).reshape(count, -1, LANES)
        else:
            out_refs[0][:, columns] = update[: count // 2]
            out_refs[1][:, columns] = rounded(update[count // 2 :])


def result_body(arrived_ref, own_ref, other_ref, out_ref):
    count, half_width = arrived_ref.shape[0], own_ref.shape[1]
    terms = widened(arrived_ref[...].reshape(count, half_width))
    of_first = lax.broadcasted_iota(jnp.int32, (count, 1), 0) % 2 == 0
    is_first = lax.axis_index("expert") % 2 == 0
    own, other = own_ref[...], other_ref[...]
    out_ref[:, :half_width] = jnp.where(is_first, own, other) + jnp.sum(
        jnp.where(of_first, terms, 0.0), axis=0, keepdims=True
    )
    out_ref[:, half_width:] = jnp.where(is_first, other, own) + jnp.sum(
        jnp.where(of_first, 0.0, terms), axis=0, keepdims=True
    )


def dense_steps(hidden_in, norm_gain, expert_ids, gate_levels, w_gate_up, w_down):
    rack_count = lax.axis_size("rack")
    group_count = lax.axis_size("expert")
    core_rows = rack_count // 2 * group_count
    token_count = 2 * core_rows
    model_width = hidden_in.shape[1]
    half_width = model_width // 2
    part_width = w_down.shape[2]
    product_width = 2 * part_width
    product_flops = 2 * token_count * half_width * product_width

    block_shape = (half_width // LANES + 2, LANES)
    sources = [hidden_in, expert_ids, gate_levels, norm_gain.reshape(-1, LANES)]
    own, other, gain_half = kernel_call(
        message_body,
        [
            in_vmem(block_shape, jnp.bfloat16),
            in_vmem(block_shape, jnp.bfloat16),
            in_vmem((1, half_width), jnp.float32),
        ],
        [],
        in_hbm=sources,
        scratch=[*(in_vmem(a.shape, a.dtype) for a in sources), pltpu.SemaphoreType.DMA((len(sources),))],
    )
    block = next(b for b in (128, 16, half_width) if half_width % b == 0)
    (gate_up_weight,) = kernel_call(
        weights_body,
        [in_vmem((half_width, product_width), jnp.bfloat16)],
        [],
        in_hbm=[w_gate_up[0, 0]],
        scratch=[
            in_vmem((half_width, 2, part_width), jnp.bfloat16),
            pltpu.SemaphoreType.DMA((half_width // block,)),
        ],
        limit=12,
    )

    def joined(ready, pieces, count):
        out_shape = [in_vmem((count,) + block_shape, jnp.bfloat16)]
        return kernel_call(joined_body, out_shape, [ready, *pieces])[0]

    near, far = gather_masks(rack_count, group_count)
    rows = [own] + [exchanged_both(other if group else own, rack, group) for rack, group in near[1:]]
    rows = joined(gate_up_weight, rows, len(near))
    rows = [rows] + [exchanged_both(rows, rack, group) for rack, group in far[1:]]
    rows = joined(gate_up_weight, rows, core_rows)
    gathered = [rows, exchanged(rows, "rack", 1)]

    piece_width = product_width // PIECES
    for step_index in range(STEPS):
        last = step_index == STEPS - 1
        product_shape = in_vmem((token_count, piece_width), jnp.float32)
        kept = [in_vmem((token_count, half_width), jnp.float32)]
        if step_index == 0:
            operands = gathered
            kept += [in_vmem((token_count, LANES), jnp.float32)]
        else:
            operands = [residual, sent, received]
        if last:
            kept = [in_vmem((1, half_width), jnp.float32)] * 2
        *kept, scaled, product, message = kernel_call(
            functools.partial(first_piece_body, step_index, rack_count, group_count),
            [
                *kept,
                in_vmem((token_count, half_width), jnp.bfloat16),
                product_shape,
                in_vmem((token_count, piece_width + LANES), jnp.bfloat16),
            ],
            operands + [gain_half, gate_up_weight],
            product_flops // PIECES,
        )
        if step_index == 0:
            residual, mixing = kept
        else:
            residual = kept[0]
        products, swapped = [product], [exchanged(message, "expert", 1)]
        for piece in range(1, PIECES):
            product, piece_message = kernel_call(
                functools.partial(other_piece_body, piece),
                [product_shape, in_vmem((token_count, piece_width), jnp.bfloat16)],
                [scaled, gate_up_weight],
                product_flops // PIECES,
            )
            products.append(product)
            swapped.append(exchanged(piece_message, "expert", 1))
        if last:
            own_row, other_row = kept
            other_row = exchanged(other_row, "expert", 1)
        updates = []
        for piece in range(PIECES):
            if piece < PIECES - 1:
                shapes = [in_vmem((token_count, half_width), jnp.float32)]
            elif last:
                shapes = [in_vmem((token_count, half_width // LANES, LANES), jnp.bfloat16)]
            else:
                shapes = [
                    in_vmem((core_rows, half_width), jnp.float32),
                    in_vmem((core_rows, half_width), jnp.bfloat16),
                ]
            updates = kernel_call(
                functools.partial(down_body, step_index, piece, model_width, group_count),
                shapes,
                [message, swapped[0], products[piece], swapped[piece], mixing, w_down[0, 0], *updates],
                product_flops // 2 // PIECES,
            )
        if last:
            updates = lax.optimization_barrier((updates[0], other_row))
            break
        update = updates[0] + widened(exchanged(updates[1], "rack", 1))
        sent = rounded(update)
        update = widened(sent)
        for mask in range(2, rack_count, 2):
            update = update + widened(exchanged(sent, "rack", mask))
        sent = rounded(update)
        update = widened(sent)
        for mask in range(2, group_count, 2):
            update = update + widened(exchanged(sent, "expert", mask))
        sent = rounded(update)
        received = exchanged(sent, "rack", 1)

    arrived = lax.all_to_all(updates[0], ("rack", "expert"), split_axis=0, concat_axis=0, tiled=True)
    (result,) = kernel_call(
        result_body, [jax.ShapeDtypeStruct((1, model_width), jnp.float32)], [arrived, own_row, updates[1]]
    )
    return result


def per_device(hidden_in, norm_gain, expert_ids, gate_levels, w_gate_up, w_down):
    rack_count = lax.axis_size("rack")
    group_count = lax.axis_size("expert")
    group_index = lax.axis_index("expert")
    half_index = group_index % 2
    tok_rows = hidden_in.shape[0]
    rack_rows = tok_rows * group_count
    slot_count = min(rack_rows, 3 * rack_rows * TOP // (2 * rack_count))
    model_width = hidden_in.shape[1]
    half_width = model_width // 2
    part_width = w_down.shape[2]
    gate_up_weight = w_gate_up[0, 0].reshape(half_width, 2 * part_width)
    down_weight = w_down[0, 0]
    all_ids, all_levels = (
        lax.all_gather(expert_ids, "expert", axis=1, tiled=True),
        lax.all_gather(gate_levels, "expert", axis=1, tiled=True),
    )
    expert_range = jnp.arange(rack_count, dtype=jnp.int32)
    slot_ids = jnp.arange(slot_count, dtype=jnp.int32)
    residual = hidden_in.astype(jnp.float32)
    for step_index in range(STEPS):
        mean_square = jnp.mean(residual * residual, axis=-1, keepdims=True)
        normed = (residual * lax.rsqrt(mean_square + 1e-06) * norm_gain).astype(jnp.bfloat16)
        rack_normed = lax.all_gather(normed, "expert", axis=0, tiled=True)
        picked = all_ids[step_index]
        level_vals = all_levels[step_index].astype(jnp.float32)
        shares = level_vals / jnp.sum(level_vals, axis=-1, keepdims=True)
        matches = picked[:, :, None] == expert_range[None, None, :]
        chosen = jnp.sum(matches.astype(jnp.int32), axis=1)
        mixing = jnp.sum(jnp.where(matches, shares[:, :, None], jnp.float32(0.0)), axis=1).astype(
            jnp.bfloat16
        )
        slot_rank = jnp.cumsum(chosen, axis=0) - chosen
        placement = chosen[:, :, None] * (slot_rank[:, :, None] == slot_ids).astype(jnp.int32)
        dispatch_map = (
            jnp.transpose(placement, (1, 2, 0))
            .reshape(rack_count * slot_count, rack_rows)
            .astype(jnp.bfloat16)
        )
        outgoing = jnp.dot(dispatch_map, rack_normed, preferred_element_type=jnp.float32).astype(
            jnp.bfloat16
        )
        outgoing = outgoing.reshape(rack_count, slot_count, model_width)
        combine_map = (placement.astype(jnp.bfloat16) * mixing[:, :, None]).reshape(
            rack_rows, rack_count * slot_count
        )
        half_rows = lax.dynamic_slice_in_dim(outgoing, half_index * half_width, half_width, 2)
        slot_rows = lax.all_to_all(half_rows, "rack", split_axis=0, concat_axis=0, tiled=True)
        layout = slot_rows.shape
        flat_rows = slot_rows.reshape(-1, half_width)
        gate_up = jnp.dot(flat_rows, gate_up_weight, preferred_element_type=jnp.float32)
        gate_up = gate_up + swapped(gate_up.astype(jnp.bfloat16), "expert", 0).astype(gate_up.dtype)
        activated = (jax.nn.silu(gate_up[:, :part_width]) * gate_up[:, part_width:]).astype(
            jnp.bfloat16
        )
        partial_value = jnp.dot(activated, down_weight, preferred_element_type=jnp.float32).astype(
            jnp.bfloat16
        )
        partial_value = partial_value.reshape(layout)
        finished = lax.all_to_all(partial_value, "rack", split_axis=0, concat_axis=0, tiled=True)
        partial_sum = jnp.dot(
            combine_map, finished.reshape(-1, half_width), preferred_element_type=jnp.float32
        )
        full_sum = jnp.zeros((rack_rows, model_width), jnp.float32)
        full_sum = lax.dynamic_update_slice_in_dim(
            full_sum, partial_sum, half_index * half_width, 1
        )
        update = lax.psum_scatter(
            full_sum.astype(jnp.bfloat16), "expert", scatter_dimension=0, tiled=True
        ).astype(jnp.float32)
        residual = residual + update
    return residual


def solution(mesh):
    in_specs = (
        P(("rack", "expert"), None),
        P(),
        P(None, ("rack", "expert"), None),
        P(None, ("rack", "expert"), None),
        P("rack", "expert", None, None, None),
        P("rack", "expert", None, None),
    )
    out_specs = P(("rack", "expert"), None)
    dense = mesh.shape["rack"] <= TOP
    return jax.shard_map(
        dense_steps if dense else per_device, mesh=mesh, in_specs=in_specs, out_specs=out_specs, check_vma=False
    )
```

```python
import functools

import jax
import jax.numpy as jnp
from jax import lax
from jax.experimental import pallas as pl
from jax.experimental.pallas import tpu as pltpu
from jax.sharding import PartitionSpec as P

TOP = 8
STEPS = 4


def swapped(shard, axis, bit):
    return lax.ppermute(shard, axis, [(i, i ^ 1 << bit) for i in range(lax.axis_size(axis))])


def exchanged(shard, axis, mask):
    return lax.ppermute(shard, axis, [(i, i ^ mask) for i in range(lax.axis_size(axis))])


def widened(values):
    return values.astype(jnp.float32)


def rounded(values):
    return values.astype(jnp.bfloat16)


def exchanged_both(shard, rack_mask, expert_mask):
    groups = lax.axis_size("expert")
    pairs = [
        (rack * groups + group, (rack ^ rack_mask) * groups + (group ^ expert_mask))
        for rack in range(lax.axis_size("rack"))
        for group in range(groups)
    ]
    return lax.ppermute(shard, ("rack", "expert"), pairs)


def crossed(rack_mask, expert_mask):
    changed = bin(rack_mask >> 1).count("1") + bin(expert_mask >> 1).count("1")
    return rack_mask ^ changed % 2, expert_mask


def gather_masks(rack_count, group_count):
    near = [(0, 0), (2, 0), (1, 1), (3, 1)]
    far = [crossed(rack, group) for group in range(0, group_count, 2) for rack in range(0, rack_count, 4)]
    return near, far


WHOLE = pl.BlockSpec(memory_space=pltpu.VMEM)
IN_HBM = pl.BlockSpec(memory_space=pltpu.HBM)
LANES = 128
PIECES = 2


def in_vmem(shape, dtype):
    return pltpu.VMEM(shape, dtype)


def kernel_call(body, out_shape, operands, flops=0, in_hbm=(), scratch=(), limit=4):
    operands = [pltpu.with_memory_space_constraint(o, pltpu.VMEM) for o in operands]
    in_hbm = [pltpu.with_memory_space_constraint(o, pltpu.HBM) for o in in_hbm]
    read = sum(o.size * o.dtype.itemsize for o in [*operands, *in_hbm])
    return pl.pallas_call(
        body,
        out_shape=out_shape,
        in_specs=[WHOLE] * len(operands) + [IN_HBM] * len(in_hbm),
        out_specs=[WHOLE] * len(out_shape),
        scratch_shapes=scratch,
        compiler_params=pltpu.CompilerParams(vmem_limit_bytes=limit * 2**20),
        cost_estimate=pl.CostEstimate(flops=flops, bytes_accessed=read, transcendentals=0),
    )(*operands, *in_hbm)


def column_blocks(width):
    block = next(b for b in (512, 256, 128, width) if width % b == 0)
    return [slice(start, start + block) for start in range(0, width, block)]


def row_blocks(values, start, stop):
    return [values[:, at : at + LANES] for at in range(start, stop, LANES)]


def message_body(hidden_in, ids_in, levels_in, gain_in, own_ref, other_ref, gain_ref, hidden, ids, levels, gain, semaphores):
    copies = [
        pltpu.make_async_copy(source, target, semaphores.at[k])
        for k, (source, target) in enumerate(
            [(hidden_in, hidden), (ids_in, ids), (levels_in, levels), (gain_in, gain)]
        )
    ]
    for copy in copies:
        copy.start()
    for copy in copies:
        copy.wait()
    half_width = hidden.shape[1] // 2
    half_rows = half_width // LANES
    is_first = lax.axis_index("expert") % 2 == 0
    row = lax.broadcasted_iota(jnp.int32, own_ref.shape, 0)

    def route_row(ref):
        values = [widened(ref[step]) for step in range(ref.shape[0])]
        used = len(values) * values[0].shape[1]
        return jnp.concatenate(values + [jnp.zeros((1, LANES - used), jnp.float32)], axis=1)

    routing = [route_row(ids), route_row(levels)]
    features = widened(hidden[...])
    first = row_blocks(features, 0, half_width)
    second = row_blocks(features, half_width, 2 * half_width)
    for target, pairs in ((own_ref, zip(first, second)), (other_ref, zip(second, first))):
        message = jnp.zeros(own_ref.shape, jnp.float32)
        for place, values in enumerate([jnp.where(is_first, a, b) for a, b in pairs] + routing):
            message = jnp.where(row == place, values, message)
        target[...] = rounded(message)
    for place in range(half_rows):
        gain_ref[:, place * LANES : (place + 1) * LANES] = jnp.where(
            is_first, gain[place : place + 1], gain[half_rows + place : half_rows + place + 1]
        )


def weights_body(*refs, first, before):
    gate_up_ref, weight_ref, arrived_ref, semaphores = refs[before:]
    part = arrived_ref.shape[2]
    count = semaphores.shape[0]
    block = arrived_ref.shape[0] // count
    blocks = [pl.ds(k * block, block) for k in range(count)]
    copies = [
        pltpu.make_async_copy(
            gate_up_ref.at[pl.ds(first + k * block, block)], arrived_ref.at[rows], semaphores.at[k]
        )
        for k, rows in enumerate(blocks)
    ]
    for copy in copies:
        copy.start()
    for copy, rows in zip(copies, blocks):
        copy.wait()
        weight_ref[rows] = arrived_ref[rows].reshape(block, 2 * part)


def joined_body(piece_count, *refs):
    pieces, out_ref = refs[:piece_count], refs[-1]
    size = out_ref.shape[0] // len(pieces)
    for k, piece in enumerate(pieces):
        out_ref[k * size : (k + 1) * size] = piece[...].reshape(size, *out_ref.shape[1:])


def own_core_of():
    rack, group = lax.axis_index("rack"), lax.axis_index("expert") // 2
    bits = [rack // 2**k for k in range(lax.axis_size("rack").bit_length() - 1)]
    bits += [group // 2**k for k in range(lax.axis_size("expert").bit_length() - 2)]
    return sum(bits) % 2


def own_place_of(core_rows, group_count):
    rack = lax.axis_index("rack")
    return (rack + own_core_of()) % 2 * core_rows + rack // 2 * group_count + lax.axis_index("expert")


def placed(gathered_refs, half_width, rack_count, group_count):
    wide = jnp.concatenate([ref[...].reshape(ref.shape[0], -1) for ref in gathered_refs], axis=0)
    count = wide.shape[0]
    place = lax.broadcasted_iota(jnp.int32, (count, count), 0)
    source = lax.broadcasted_iota(jnp.int32, (count, count), 1)
    near, far = gather_masks(rack_count, group_count)
    distance = source // (count // 2) * (count // 2)
    for masks, index in ((near, source % len(near)), (far, source // len(near) % len(far))):
        for k, (rack, group) in enumerate(masks):
            step = rack % 2 * (count // 2) + rack // 2 * group_count + group
            distance = distance ^ jnp.where(index == k, step, 0)
    own_place = own_place_of(count // 2, group_count)
    to_place = rounded(jnp.where(place == (distance ^ own_place), 1.0, 0.0))
    wide = jnp.dot(to_place, wide, preferred_element_type=jnp.float32)
    residual = wide[:, :half_width]
    ids = wide[:, half_width : half_width + LANES]
    levels = wide[:, half_width + LANES : half_width + 2 * LANES]
    lane = lax.broadcasted_iota(jnp.int32, ids.shape, 1)
    chosen = ids == lax.axis_index("rack").astype(jnp.float32)
    mixing = jnp.zeros(ids.shape, jnp.float32)
    for step in range(STEPS):
        of_step = lane // TOP == step
        total = jnp.sum(jnp.where(of_step, levels, 0.0), axis=1, keepdims=True)
        share = jnp.sum(jnp.where(of_step & chosen, levels / total, 0.0), axis=1, keepdims=True)
        mixing = jnp.where(lane == step, widened(rounded(share)), mixing)
    return residual, mixing


def piece_columns(piece, part):
    size = part // PIECES
    return [slice(start, start + size) for start in (piece * size, part + piece * size)]


def multiplied(scaled, upper_ref, lower_ref, piece, product_ref, message_ref):
    depth, width = upper_ref.shape
    size = width // 2 // PIECES
    for k, columns in enumerate(piece_columns(piece, width // 2)):
        product = jnp.dot(scaled[:, :depth], upper_ref[:, columns], preferred_element_type=jnp.float32)
        product += jnp.dot(scaled[:, depth:], lower_ref[:, columns], preferred_element_type=jnp.float32)
        product_ref[:, k * size : (k + 1) * size] = product
        message_ref[:, k * size : (k + 1) * size] = rounded(product)


def first_piece_body(step, rack_count, group_count, *refs):
    first, last = step == 0, step == STEPS - 1
    if first:
        *gathered_refs, gain_ref, upper_ref, lower_ref, residual_ref, mixing_ref, scaled_ref, product_ref, message_ref = refs
        residual, mixing_ref[...] = placed(gathered_refs, gain_ref.shape[1], rack_count, group_count)
        residual_ref[...] = residual
    else:
        before_ref, own_ref, other_ref, gain_ref, upper_ref, lower_ref, *residual_refs, scaled_ref, product_ref, message_ref = refs
        update = jnp.concatenate([own_ref[...], other_ref[...]], axis=0)
        residual = before_ref[...] + widened(update)
        if last:
            place = lax.broadcasted_iota(jnp.int32, (residual.shape[0], 1), 0)
            own_place = own_place_of(residual.shape[0] // 2, group_count)
            for ref, wanted in zip(residual_refs, (own_place, own_place ^ 1)):
                ref[...] = jnp.sum(jnp.where(place == wanted, residual, 0.0), axis=0, keepdims=True)
        else:
            residual_refs[0][...] = residual
    scaled = rounded(residual * gain_ref[...])
    scaled_ref[...] = scaled
    multiplied(scaled, upper_ref, lower_ref, 0, product_ref, message_ref)
    square_sum = jnp.sum(residual * residual, axis=1, keepdims=True)
    square_high = widened(rounded(square_sum))
    lane = lax.broadcasted_iota(jnp.int32, (residual.shape[0], LANES), 1)
    tail = jnp.where(lane == 0, square_high, square_sum - square_high)
    message_ref[:, product_ref.shape[1] :] = rounded(tail)


def other_piece_body(piece, scaled_ref, upper_ref, lower_ref, product_ref, message_ref):
    multiplied(scaled_ref[...], upper_ref, lower_ref, piece, product_ref, message_ref)


def token_matrix(count, group_count):
    token = lax.broadcasted_iota(jnp.int32, (count, count), 0)
    place = lax.broadcasted_iota(jnp.int32, (count, count), 1)
    rack = token // group_count
    core = (rack + own_core_of()) % 2
    matches = core * (count // 2) + rack // 2 * group_count + token % group_count == place
    return rounded(jnp.where(matches, 1.0, 0.0))


def down_body(step, piece, model_width, group_count, tail_ref, other_tail_ref, product_ref, swapped_ref, mixing_ref, weight_ref, *refs):
    width = product_ref.shape[1]
    size = width // 2
    tails = widened(tail_ref[:, width:]) + widened(other_tail_ref[:, width:])
    square_sum = tails[:, 0:1] + tails[:, 1:2]
    scale = lax.rsqrt(square_sum / model_width + 1e-06)
    whole = product_ref[...] + widened(swapped_ref[:, :width])
    gate = whole[:, :size] * scale
    up = whole[:, size:] * scale
    activated = rounded(gate / (1.0 + jnp.exp(-gate)) * up)
    mixing = mixing_ref[...]
    count = mixing.shape[0]
    last = step == STEPS - 1
    if last:
        to_tokens = token_matrix(count, group_count)
        activated = rounded(jnp.dot(to_tokens, activated, preferred_element_type=jnp.float32))
        mixing = jnp.dot(to_tokens, rounded(mixing), preferred_element_type=jnp.float32)
    mixing = mixing[:, step : step + 1]
    rows = slice(piece * size, (piece + 1) * size)
    before_refs, out_refs = (refs[:1], refs[1:]) if piece else ((), refs)
    for columns in column_blocks(weight_ref.shape[1]):
        term = jnp.dot(activated, weight_ref[rows, columns], preferred_element_type=jnp.float32)
        for ref in before_refs:
            term = term + ref[:, columns]
        if piece < PIECES - 1:
            out_refs[0][:, columns] = term
            continue
        update = widened(rounded(term)) * mixing
        if last:
            blocks = slice(columns.start // LANES, columns.stop // LANES)
            out_refs[0][:, blocks] = rounded(update).reshape(count, -1, LANES)
        else:
            out_refs[0][:, columns] = update[: count // 2]
            out_refs[1][:, columns] = rounded(update[count // 2 :])


def result_body(arrived_ref, own_ref, other_ref, out_ref):
    count, half_width = arrived_ref.shape[0], own_ref.shape[1]
    terms = widened(arrived_ref[...].reshape(count, half_width))
    of_first = lax.broadcasted_iota(jnp.int32, (count, 1), 0) % 2 == 0
    is_first = lax.axis_index("expert") % 2 == 0
    own, other = own_ref[...], other_ref[...]
    out_ref[:, :half_width] = jnp.where(is_first, own, other) + jnp.sum(
        jnp.where(of_first, terms, 0.0), axis=0, keepdims=True
    )
    out_ref[:, half_width:] = jnp.where(is_first, other, own) + jnp.sum(
        jnp.where(of_first, 0.0, terms), axis=0, keepdims=True
    )


def dense_steps(hidden_in, norm_gain, expert_ids, gate_levels, w_gate_up, w_down):
    rack_count = lax.axis_size("rack")
    group_count = lax.axis_size("expert")
    core_rows = rack_count // 2 * group_count
    token_count = 2 * core_rows
    model_width = hidden_in.shape[1]
    half_width = model_width // 2
    part_width = w_down.shape[2]
    product_width = 2 * part_width
    product_flops = 2 * token_count * half_width * product_width

    block_shape = (half_width // LANES + 2, LANES)
    sources = [hidden_in, expert_ids, gate_levels, norm_gain.reshape(-1, LANES)]
    own, other, gain_half = kernel_call(
        message_body,
        [
            in_vmem(block_shape, jnp.bfloat16),
            in_vmem(block_shape, jnp.bfloat16),
            in_vmem((1, half_width), jnp.float32),
        ],
        [],
        in_hbm=sources,
        scratch=[*(in_vmem(a.shape, a.dtype) for a in sources), pltpu.SemaphoreType.DMA((len(sources),))],
    )
    block = next(b for b in (128, 16, half_width) if half_width % b == 0)

    def turned(start, stop, *before):
        return kernel_call(
            functools.partial(weights_body, first=start, before=len(before)),
            [in_vmem((stop - start, product_width), jnp.bfloat16)],
            before,
            in_hbm=[w_gate_up[0, 0]],
            scratch=[
                in_vmem((stop - start, 2, part_width), jnp.bfloat16),
                pltpu.SemaphoreType.DMA(((stop - start) // block,)),
            ],
            limit=12,
        )[0]

    def joined(pieces, count, *before):
        out_shape = [in_vmem((count,) + block_shape, jnp.bfloat16)]
        return kernel_call(functools.partial(joined_body, len(pieces)), out_shape, [*pieces, *before])[0]

    near, far = gather_masks(rack_count, group_count)
    middle = -(-half_width // 2 // 256) * 256
    upper = turned(0, middle)
    rows = [own] + [exchanged_both(other if group else own, rack, group) for rack, group in near[1:]]
    rows = joined(rows, len(near), upper)
    lower = turned(middle, half_width, rows)
    gate_up_weights = [upper, lower]
    rows = [rows] + [exchanged_both(rows, rack, group) for rack, group in far[1:]]
    rows = joined(rows, core_rows, lower)
    gathered = [rows, exchanged(rows, "rack", 1)]

    piece_width = product_width // PIECES
    for step_index in range(STEPS):
        last = step_index == STEPS - 1
        product_shape = in_vmem((token_count, piece_width), jnp.float32)
        kept = [in_vmem((token_count, half_width), jnp.float32)]
        if step_index == 0:
            operands = gathered
            kept += [in_vmem((token_count, LANES), jnp.float32)]
        else:
            operands = [residual, sent, received]
        if last:
            kept = [in_vmem((1, half_width), jnp.float32)] * 2
        *kept, scaled, product, message = kernel_call(
            functools.partial(first_piece_body, step_index, rack_count, group_count),
            [
                *kept,
                in_vmem((token_count, half_width), jnp.bfloat16),
                product_shape,
                in_vmem((token_count, piece_width + LANES), jnp.bfloat16),
            ],
            operands + [gain_half, *gate_up_weights],
            product_flops // PIECES,
        )
        if step_index == 0:
            residual, mixing = kept
        else:
            residual = kept[0]
        products, swapped = [product], [exchanged(message, "expert", 1)]
        for piece in range(1, PIECES):
            product, piece_message = kernel_call(
                functools.partial(other_piece_body, piece),
                [product_shape, in_vmem((token_count, piece_width), jnp.bfloat16)],
                [scaled, *gate_up_weights],
                product_flops // PIECES,
            )
            products.append(product)
            swapped.append(exchanged(piece_message, "expert", 1))
        if last:
            own_row, other_row = kept
            other_row = exchanged(other_row, "expert", 1)
        updates = []
        for piece in range(PIECES):
            if piece < PIECES - 1:
                shapes = [in_vmem((token_count, half_width), jnp.float32)]
            elif last:
                shapes = [in_vmem((token_count, half_width // LANES, LANES), jnp.bfloat16)]
            else:
                shapes = [
                    in_vmem((core_rows, half_width), jnp.float32),
                    in_vmem((core_rows, half_width), jnp.bfloat16),
                ]
            updates = kernel_call(
                functools.partial(down_body, step_index, piece, model_width, group_count),
                shapes,
                [message, swapped[0], products[piece], swapped[piece], mixing, w_down[0, 0], *updates],
                product_flops // 2 // PIECES,
            )
        if last:
            updates = lax.optimization_barrier((updates[0], other_row))
            break
        update = updates[0] + widened(exchanged(updates[1], "rack", 1))
        sent = rounded(update)
        update = widened(sent)
        for mask in range(2, rack_count, 2):
            update = update + widened(exchanged_both(sent, *crossed(mask, 0)))
        sent = rounded(update)
        update = widened(sent)
        for mask in range(2, group_count, 2):
            update = update + widened(exchanged_both(sent, *crossed(0, mask)))
        sent = rounded(update)
        received = exchanged(sent, "rack", 1)

    arrived = lax.all_to_all(updates[0], ("rack", "expert"), split_axis=0, concat_axis=0, tiled=True)
    (result,) = kernel_call(
        result_body, [jax.ShapeDtypeStruct((1, model_width), jnp.float32)], [arrived, own_row, updates[1]]
    )
    return result


def per_device(hidden_in, norm_gain, expert_ids, gate_levels, w_gate_up, w_down):
    rack_count = lax.axis_size("rack")
    group_count = lax.axis_size("expert")
    group_index = lax.axis_index("expert")
    half_index = group_index % 2
    tok_rows = hidden_in.shape[0]
    rack_rows = tok_rows * group_count
    slot_count = min(rack_rows, 3 * rack_rows * TOP // (2 * rack_count))
    model_width = hidden_in.shape[1]
    half_width = model_width // 2
    part_width = w_down.shape[2]
    gate_up_weight = w_gate_up[0, 0].reshape(half_width, 2 * part_width)
    down_weight = w_down[0, 0]
    all_ids, all_levels = (
        lax.all_gather(expert_ids, "expert", axis=1, tiled=True),
        lax.all_gather(gate_levels, "expert", axis=1, tiled=True),
    )
    expert_range = jnp.arange(rack_count, dtype=jnp.int32)
    slot_ids = jnp.arange(slot_count, dtype=jnp.int32)
    residual = hidden_in.astype(jnp.float32)
    for step_index in range(STEPS):
        mean_square = jnp.mean(residual * residual, axis=-1, keepdims=True)
        normed = (residual * lax.rsqrt(mean_square + 1e-06) * norm_gain).astype(jnp.bfloat16)
        rack_normed = lax.all_gather(normed, "expert", axis=0, tiled=True)
        picked = all_ids[step_index]
        level_vals = all_levels[step_index].astype(jnp.float32)
        shares = level_vals / jnp.sum(level_vals, axis=-1, keepdims=True)
        matches = picked[:, :, None] == expert_range[None, None, :]
        chosen = jnp.sum(matches.astype(jnp.int32), axis=1)
        mixing = jnp.sum(jnp.where(matches, shares[:, :, None], jnp.float32(0.0)), axis=1).astype(
            jnp.bfloat16
        )
        slot_rank = jnp.cumsum(chosen, axis=0) - chosen
        placement = chosen[:, :, None] * (slot_rank[:, :, None] == slot_ids).astype(jnp.int32)
        dispatch_map = (
            jnp.transpose(placement, (1, 2, 0))
            .reshape(rack_count * slot_count, rack_rows)
            .astype(jnp.bfloat16)
        )
        outgoing = jnp.dot(dispatch_map, rack_normed, preferred_element_type=jnp.float32).astype(
            jnp.bfloat16
        )
        outgoing = outgoing.reshape(rack_count, slot_count, model_width)
        combine_map = (placement.astype(jnp.bfloat16) * mixing[:, :, None]).reshape(
            rack_rows, rack_count * slot_count
        )
        half_rows = lax.dynamic_slice_in_dim(outgoing, half_index * half_width, half_width, 2)
        slot_rows = lax.all_to_all(half_rows, "rack", split_axis=0, concat_axis=0, tiled=True)
        layout = slot_rows.shape
        flat_rows = slot_rows.reshape(-1, half_width)
        gate_up = jnp.dot(flat_rows, gate_up_weight, preferred_element_type=jnp.float32)
        gate_up = gate_up + swapped(gate_up.astype(jnp.bfloat16), "expert", 0).astype(gate_up.dtype)
        activated = (jax.nn.silu(gate_up[:, :part_width]) * gate_up[:, part_width:]).astype(
            jnp.bfloat16
        )
        partial_value = jnp.dot(activated, down_weight, preferred_element_type=jnp.float32).astype(
            jnp.bfloat16
        )
        partial_value = partial_value.reshape(layout)
        finished = lax.all_to_all(partial_value, "rack", split_axis=0, concat_axis=0, tiled=True)
        partial_sum = jnp.dot(
            combine_map, finished.reshape(-1, half_width), preferred_element_type=jnp.float32
        )
        full_sum = jnp.zeros((rack_rows, model_width), jnp.float32)
        full_sum = lax.dynamic_update_slice_in_dim(
            full_sum, partial_sum, half_index * half_width, 1
        )
        update = lax.psum_scatter(
            full_sum.astype(jnp.bfloat16), "expert", scatter_dimension=0, tiled=True
        ).astype(jnp.float32)
        residual = residual + update
    return residual


def solution(mesh):
    in_specs = (
        P(("rack", "expert"), None),
        P(),
        P(None, ("rack", "expert"), None),
        P(None, ("rack", "expert"), None),
        P("rack", "expert", None, None, None),
        P("rack", "expert", None, None),
    )
    out_specs = P(("rack", "expert"), None)
    dense = mesh.shape["rack"] <= TOP
    return jax.shard_map(
        dense_steps if dense else per_device, mesh=mesh, in_specs=in_specs, out_specs=out_specs, check_vma=False
    )
```

```python
import functools

import jax
import jax.numpy as jnp
from jax import lax
from jax.experimental import pallas as pl
from jax.experimental.pallas import tpu as pltpu
from jax.sharding import PartitionSpec as P

TOP = 8
STEPS = 4


def swapped(shard, axis, bit):
    return lax.ppermute(shard, axis, [(i, i ^ 1 << bit) for i in range(lax.axis_size(axis))])


def exchanged(shard, axis, mask):
    return lax.ppermute(shard, axis, [(i, i ^ mask) for i in range(lax.axis_size(axis))])


def widened(values):
    return values.astype(jnp.float32)


def rounded(values):
    return values.astype(jnp.bfloat16)


def exchanged_both(shard, rack_mask, expert_mask):
    groups = lax.axis_size("expert")
    pairs = [
        (rack * groups + group, (rack ^ rack_mask) * groups + (group ^ expert_mask))
        for rack in range(lax.axis_size("rack"))
        for group in range(groups)
    ]
    return lax.ppermute(shard, ("rack", "expert"), pairs)


def crossed(rack_mask, expert_mask):
    changed = bin(rack_mask >> 1).count("1") + bin(expert_mask >> 1).count("1")
    return rack_mask ^ changed % 2, expert_mask


def gather_masks(rack_count, group_count):
    near = [(0, 0), (2, 0), (1, 1), (3, 1)]
    far = [crossed(rack, group) for group in range(0, group_count, 2) for rack in range(0, rack_count, 4)]
    return near, far


WHOLE = pl.BlockSpec(memory_space=pltpu.VMEM)
IN_HBM = pl.BlockSpec(memory_space=pltpu.HBM)
LANES = 128
PIECES = 2


def in_vmem(shape, dtype):
    return pltpu.VMEM(shape, dtype)


def kernel_call(body, out_shape, operands, flops=0, in_hbm=(), scratch=(), limit=4):
    operands = [pltpu.with_memory_space_constraint(o, pltpu.VMEM) for o in operands]
    in_hbm = [pltpu.with_memory_space_constraint(o, pltpu.HBM) for o in in_hbm]
    read = sum(o.size * o.dtype.itemsize for o in [*operands, *in_hbm])
    return pl.pallas_call(
        body,
        out_shape=out_shape,
        in_specs=[WHOLE] * len(operands) + [IN_HBM] * len(in_hbm),
        out_specs=[WHOLE] * len(out_shape),
        scratch_shapes=scratch,
        compiler_params=pltpu.CompilerParams(vmem_limit_bytes=limit * 2**20),
        cost_estimate=pl.CostEstimate(flops=flops, bytes_accessed=read, transcendentals=0),
    )(*operands, *in_hbm)


def column_blocks(width):
    block = next(b for b in (512, 256, 128, width) if width % b == 0)
    return [slice(start, start + block) for start in range(0, width, block)]


def row_blocks(values, start, stop):
    return [values[:, at : at + LANES] for at in range(start, stop, LANES)]


def message_body(hidden_in, ids_in, levels_in, gain_in, own_ref, other_ref, gain_ref, hidden, ids, levels, gain, semaphores):
    copies = [
        pltpu.make_async_copy(source, target, semaphores.at[k])
        for k, (source, target) in enumerate(
            [(hidden_in, hidden), (ids_in, ids), (levels_in, levels), (gain_in, gain)]
        )
    ]
    for copy in copies:
        copy.start()
    for copy in copies:
        copy.wait()
    half_width = hidden.shape[1] // 2
    half_rows = half_width // LANES
    is_first = lax.axis_index("expert") % 2 == 0
    row = lax.broadcasted_iota(jnp.int32, own_ref.shape, 0)

    def route_row(ref):
        values = [widened(ref[step]) for step in range(ref.shape[0])]
        used = len(values) * values[0].shape[1]
        return jnp.concatenate(values + [jnp.zeros((1, LANES - used), jnp.float32)], axis=1)

    routing = [route_row(ids), route_row(levels)]
    features = widened(hidden[...])
    first = row_blocks(features, 0, half_width)
    second = row_blocks(features, half_width, 2 * half_width)
    for target, pairs in ((own_ref, zip(first, second)), (other_ref, zip(second, first))):
        message = jnp.zeros(own_ref.shape, jnp.float32)
        for place, values in enumerate([jnp.where(is_first, a, b) for a, b in pairs] + routing):
            message = jnp.where(row == place, values, message)
        target[...] = rounded(message)
    for place in range(half_rows):
        gain_ref[:, place * LANES : (place + 1) * LANES] = jnp.where(
            is_first, gain[place : place + 1], gain[half_rows + place : half_rows + place + 1]
        )


def weights_body(*refs, first, before):
    gate_up_ref, weight_ref, arrived_ref, semaphores = refs[before:]
    part = arrived_ref.shape[2]
    count = semaphores.shape[0]
    block = arrived_ref.shape[0] // count
    blocks = [pl.ds(k * block, block) for k in range(count)]
    copies = [
        pltpu.make_async_copy(
            gate_up_ref.at[pl.ds(first + k * block, block)], arrived_ref.at[rows], semaphores.at[k]
        )
        for k, rows in enumerate(blocks)
    ]
    for copy in copies:
        copy.start()
    for copy, rows in zip(copies, blocks):
        copy.wait()
        weight_ref[rows] = arrived_ref[rows].reshape(block, 2 * part)


def joined_body(piece_count, *refs):
    pieces, out_ref = refs[:piece_count], refs[-1]
    size = out_ref.shape[0] // len(pieces)
    for k, piece in enumerate(pieces):
        out_ref[k * size : (k + 1) * size] = piece[...].reshape(size, *out_ref.shape[1:])


def own_core_of():
    rack, group = lax.axis_index("rack"), lax.axis_index("expert") // 2
    bits = [rack // 2**k for k in range(lax.axis_size("rack").bit_length() - 1)]
    bits += [group // 2**k for k in range(lax.axis_size("expert").bit_length() - 2)]
    return sum(bits) % 2


def own_place_of(core_rows, group_count):
    rack = lax.axis_index("rack")
    return (rack + own_core_of()) % 2 * core_rows + rack // 2 * group_count + lax.axis_index("expert")


def placed(gathered_refs, half_width, rack_count, group_count):
    wide = jnp.concatenate([ref[...].reshape(ref.shape[0], -1) for ref in gathered_refs], axis=0)
    count = wide.shape[0]
    place = lax.broadcasted_iota(jnp.int32, (count, count), 0)
    source = lax.broadcasted_iota(jnp.int32, (count, count), 1)
    near, far = gather_masks(rack_count, group_count)
    distance = source // (count // 2) * (count // 2)
    for masks, index in ((near, source % len(near)), (far, source // len(near) % len(far))):
        for k, (rack, group) in enumerate(masks):
            step = rack % 2 * (count // 2) + rack // 2 * group_count + group
            distance = distance ^ jnp.where(index == k, step, 0)
    own_place = own_place_of(count // 2, group_count)
    to_place = rounded(jnp.where(place == (distance ^ own_place), 1.0, 0.0))
    wide = jnp.dot(to_place, wide, preferred_element_type=jnp.float32)
    residual = wide[:, :half_width]
    ids = wide[:, half_width : half_width + LANES]
    levels = wide[:, half_width + LANES : half_width + 2 * LANES]
    lane = lax.broadcasted_iota(jnp.int32, ids.shape, 1)
    chosen = ids == lax.axis_index("rack").astype(jnp.float32)
    mixing = jnp.zeros(ids.shape, jnp.float32)
    for step in range(STEPS):
        of_step = lane // TOP == step
        total = jnp.sum(jnp.where(of_step, levels, 0.0), axis=1, keepdims=True)
        share = jnp.sum(jnp.where(of_step & chosen, levels / total, 0.0), axis=1, keepdims=True)
        mixing = jnp.where(lane == step, widened(rounded(share)), mixing)
    return residual, mixing


def piece_columns(piece, part):
    size = part // PIECES
    return [slice(start, start + size) for start in (piece * size, part + piece * size)]


def multiplied(scaled, upper_ref, lower_ref, piece, product_ref, message_ref):
    depth, width = upper_ref.shape
    size = width // 2 // PIECES
    for k, columns in enumerate(piece_columns(piece, width // 2)):
        product = jnp.dot(scaled[:, :depth], upper_ref[:, columns], preferred_element_type=jnp.float32)
        product += jnp.dot(scaled[:, depth:], lower_ref[:, columns], preferred_element_type=jnp.float32)
        product_ref[:, k * size : (k + 1) * size] = product
        message_ref[:, k * size : (k + 1) * size] = rounded(product)


def first_piece_body(step, rack_count, group_count, *refs):
    first, last = step == 0, step == STEPS - 1
    if first:
        *gathered_refs, gain_ref, upper_ref, lower_ref, residual_ref, mixing_ref, scaled_ref, product_ref, message_ref = refs
        residual, mixing_ref[...] = placed(gathered_refs, gain_ref.shape[1], rack_count, group_count)
        residual_ref[...] = residual
    else:
        before_ref, own_ref, other_ref, gain_ref, upper_ref, lower_ref, *residual_refs, scaled_ref, product_ref, message_ref = refs
        update = jnp.concatenate([own_ref[...], other_ref[...]], axis=0)
        residual = before_ref[...] + widened(update)
        if last:
            place = lax.broadcasted_iota(jnp.int32, (residual.shape[0], 1), 0)
            own_place = own_place_of(residual.shape[0] // 2, group_count)
            for ref, wanted in zip(residual_refs, (own_place, own_place ^ 1)):
                ref[...] = jnp.sum(jnp.where(place == wanted, residual, 0.0), axis=0, keepdims=True)
        else:
            residual_refs[0][...] = residual
    scaled = rounded(residual * gain_ref[...])
    scaled_ref[...] = scaled
    multiplied(scaled, upper_ref, lower_ref, 0, product_ref, message_ref)
    square_sum = jnp.sum(residual * residual, axis=1, keepdims=True)
    square_high = widened(rounded(square_sum))
    lane = lax.broadcasted_iota(jnp.int32, (residual.shape[0], LANES), 1)
    tail = jnp.where(lane == 0, square_high, square_sum - square_high)
    message_ref[:, product_ref.shape[1] :] = rounded(tail)


def other_piece_body(piece, scaled_ref, upper_ref, lower_ref, product_ref, message_ref):
    multiplied(scaled_ref[...], upper_ref, lower_ref, piece, product_ref, message_ref)


def down_body(step, piece, model_width, group_count, tail_ref, other_tail_ref, product_ref, swapped_ref, mixing_ref, weight_ref, *refs):
    width = product_ref.shape[1]
    size = width // 2
    tails = widened(tail_ref[:, width:]) + widened(other_tail_ref[:, width:])
    square_sum = tails[:, 0:1] + tails[:, 1:2]
    scale = lax.rsqrt(square_sum / model_width + 1e-06)
    whole = product_ref[...] + widened(swapped_ref[:, :width])
    gate = whole[:, :size] * scale
    up = whole[:, size:] * scale
    activated = rounded(gate / (1.0 + jnp.exp(-gate)) * up)
    mixing = mixing_ref[...]
    count = mixing.shape[0]
    last = step == STEPS - 1
    mixing = mixing[:, step : step + 1]
    rows = slice(piece * size, (piece + 1) * size)
    before_refs, out_refs = (refs[:1], refs[1:]) if piece else ((), refs)
    final = piece == PIECES - 1
    for columns in [slice(0, weight_ref.shape[1])] if last and final else column_blocks(weight_ref.shape[1]):
        term = jnp.dot(activated, weight_ref[rows, columns], preferred_element_type=jnp.float32)
        for ref in before_refs:
            term = term + ref[:, columns]
        if not final:
            out_refs[0][:, columns] = term
            continue
        update = widened(rounded(term)) * mixing
        if not last:
            out_refs[0][:, columns] = update[: count // 2]
            out_refs[1][:, columns] = rounded(update[count // 2 :])
            continue
        blocks = rounded(update).reshape(count, -1, LANES)
        for start in range(0, count, group_count):
            chip, core = start % (count // 2) // group_count, (start // (count // 2) + own_core_of()) % 2
            out_refs[0][pl.ds((2 * chip + core) * group_count, group_count)] = blocks[start : start + group_count]


def result_body(arrived_ref, own_ref, other_ref, out_ref):
    count, half_width = arrived_ref.shape[0], own_ref.shape[1]
    terms = widened(arrived_ref[...].reshape(count, half_width))
    of_first = lax.broadcasted_iota(jnp.int32, (count, 1), 0) % 2 == 0
    is_first = lax.axis_index("expert") % 2 == 0
    own, other = own_ref[...], other_ref[...]
    out_ref[:, :half_width] = jnp.where(is_first, own, other) + jnp.sum(
        jnp.where(of_first, terms, 0.0), axis=0, keepdims=True
    )
    out_ref[:, half_width:] = jnp.where(is_first, other, own) + jnp.sum(
        jnp.where(of_first, 0.0, terms), axis=0, keepdims=True
    )


def dense_steps(hidden_in, norm_gain, expert_ids, gate_levels, w_gate_up, w_down):
    rack_count = lax.axis_size("rack")
    group_count = lax.axis_size("expert")
    core_rows = rack_count // 2 * group_count
    token_count = 2 * core_rows
    model_width = hidden_in.shape[1]
    half_width = model_width // 2
    part_width = w_down.shape[2]
    product_width = 2 * part_width
    product_flops = 2 * token_count * half_width * product_width

    block_shape = (half_width // LANES + 2, LANES)
    sources = [hidden_in, expert_ids, gate_levels, norm_gain.reshape(-1, LANES)]
    own, other, gain_half = kernel_call(
        message_body,
        [
            in_vmem(block_shape, jnp.bfloat16),
            in_vmem(block_shape, jnp.bfloat16),
            in_vmem((1, half_width), jnp.float32),
        ],
        [],
        in_hbm=sources,
        scratch=[*(in_vmem(a.shape, a.dtype) for a in sources), pltpu.SemaphoreType.DMA((len(sources),))],
    )
    block = next(b for b in (128, 16, half_width) if half_width % b == 0)

    def turned(start, stop, *before):
        return kernel_call(
            functools.partial(weights_body, first=start, before=len(before)),
            [in_vmem((stop - start, product_width), jnp.bfloat16)],
            before,
            in_hbm=[w_gate_up[0, 0]],
            scratch=[
                in_vmem((stop - start, 2, part_width), jnp.bfloat16),
                pltpu.SemaphoreType.DMA(((stop - start) // block,)),
            ],
            limit=12,
        )[0]

    def joined(pieces, count, *before):
        out_shape = [in_vmem((count,) + block_shape, jnp.bfloat16)]
        return kernel_call(functools.partial(joined_body, len(pieces)), out_shape, [*pieces, *before])[0]

    near, far = gather_masks(rack_count, group_count)
    middle = -(-half_width // 2 // 256) * 256
    upper = turned(0, middle)
    rows = [own] + [exchanged_both(other if group else own, rack, group) for rack, group in near[1:]]
    rows = joined(rows, len(near), upper)
    lower = turned(middle, half_width, rows)
    gate_up_weights = [upper, lower]
    rows = [rows] + [exchanged_both(rows, rack, group) for rack, group in far[1:]]
    rows = joined(rows, core_rows, lower)
    gathered = [rows, exchanged(rows, "rack", 1)]

    piece_width = product_width // PIECES
    for step_index in range(STEPS):
        last = step_index == STEPS - 1
        product_shape = in_vmem((token_count, piece_width), jnp.float32)
        kept = [in_vmem((token_count, half_width), jnp.float32)]
        if step_index == 0:
            operands = gathered
            kept += [in_vmem((token_count, LANES), jnp.float32)]
        else:
            operands = [residual, sent, received]
        if last:
            kept = [in_vmem((1, half_width), jnp.float32)] * 2
        *kept, scaled, product, message = kernel_call(
            functools.partial(first_piece_body, step_index, rack_count, group_count),
            [
                *kept,
                in_vmem((token_count, half_width), jnp.bfloat16),
                product_shape,
                in_vmem((token_count, piece_width + LANES), jnp.bfloat16),
            ],
            operands + [gain_half, *gate_up_weights],
            product_flops // PIECES,
        )
        if step_index == 0:
            residual, mixing = kept
        else:
            residual = kept[0]
        products, swapped = [product], [exchanged(message, "expert", 1)]
        for piece in range(1, PIECES):
            product, piece_message = kernel_call(
                functools.partial(other_piece_body, piece),
                [product_shape, in_vmem((token_count, piece_width), jnp.bfloat16)],
                [scaled, *gate_up_weights],
                product_flops // PIECES,
            )
            products.append(product)
            swapped.append(exchanged(piece_message, "expert", 1))
        if last:
            own_row, other_row = kept
            other_row = exchanged(other_row, "expert", 1)
        updates = []
        for piece in range(PIECES):
            if piece < PIECES - 1:
                shapes = [in_vmem((token_count, half_width), jnp.float32)]
            elif last:
                shapes = [in_vmem((token_count, half_width // LANES, LANES), jnp.bfloat16)]
            else:
                shapes = [
                    in_vmem((core_rows, half_width), jnp.float32),
                    in_vmem((core_rows, half_width), jnp.bfloat16),
                ]
            updates = kernel_call(
                functools.partial(down_body, step_index, piece, model_width, group_count),
                shapes,
                [message, swapped[0], products[piece], swapped[piece], mixing, w_down[0, 0], *updates],
                product_flops // 2 // PIECES,
            )
        if last:
            updates = lax.optimization_barrier((updates[0], other_row))
            break
        update = updates[0] + widened(exchanged(updates[1], "rack", 1))
        sent = rounded(update)
        update = widened(sent)
        for mask in range(2, rack_count, 2):
            update = update + widened(exchanged_both(sent, *crossed(mask, 0)))
        sent = rounded(update)
        update = widened(sent)
        for mask in range(2, group_count, 2):
            update = update + widened(exchanged_both(sent, *crossed(0, mask)))
        sent = rounded(update)
        received = exchanged(sent, "rack", 1)

    arrived = lax.all_to_all(updates[0], ("rack", "expert"), split_axis=0, concat_axis=0, tiled=True)
    (result,) = kernel_call(
        result_body, [jax.ShapeDtypeStruct((1, model_width), jnp.float32)], [arrived, own_row, updates[1]]
    )
    return result


def per_device(hidden_in, norm_gain, expert_ids, gate_levels, w_gate_up, w_down):
    rack_count = lax.axis_size("rack")
    group_count = lax.axis_size("expert")
    group_index = lax.axis_index("expert")
    half_index = group_index % 2
    tok_rows = hidden_in.shape[0]
    rack_rows = tok_rows * group_count
    slot_count = min(rack_rows, 3 * rack_rows * TOP // (2 * rack_count))
    model_width = hidden_in.shape[1]
    half_width = model_width // 2
    part_width = w_down.shape[2]
    gate_up_weight = w_gate_up[0, 0].reshape(half_width, 2 * part_width)
    down_weight = w_down[0, 0]
    all_ids, all_levels = (
        lax.all_gather(expert_ids, "expert", axis=1, tiled=True),
        lax.all_gather(gate_levels, "expert", axis=1, tiled=True),
    )
    expert_range = jnp.arange(rack_count, dtype=jnp.int32)
    slot_ids = jnp.arange(slot_count, dtype=jnp.int32)
    residual = hidden_in.astype(jnp.float32)
    for step_index in range(STEPS):
        mean_square = jnp.mean(residual * residual, axis=-1, keepdims=True)
        normed = (residual * lax.rsqrt(mean_square + 1e-06) * norm_gain).astype(jnp.bfloat16)
        rack_normed = lax.all_gather(normed, "expert", axis=0, tiled=True)
        picked = all_ids[step_index]
        level_vals = all_levels[step_index].astype(jnp.float32)
        shares = level_vals / jnp.sum(level_vals, axis=-1, keepdims=True)
        matches = picked[:, :, None] == expert_range[None, None, :]
        chosen = jnp.sum(matches.astype(jnp.int32), axis=1)
        mixing = jnp.sum(jnp.where(matches, shares[:, :, None], jnp.float32(0.0)), axis=1).astype(
            jnp.bfloat16
        )
        slot_rank = jnp.cumsum(chosen, axis=0) - chosen
        placement = chosen[:, :, None] * (slot_rank[:, :, None] == slot_ids).astype(jnp.int32)
        dispatch_map = (
            jnp.transpose(placement, (1, 2, 0))
            .reshape(rack_count * slot_count, rack_rows)
            .astype(jnp.bfloat16)
        )
        outgoing = jnp.dot(dispatch_map, rack_normed, preferred_element_type=jnp.float32).astype(
            jnp.bfloat16
        )
        outgoing = outgoing.reshape(rack_count, slot_count, model_width)
        combine_map = (placement.astype(jnp.bfloat16) * mixing[:, :, None]).reshape(
            rack_rows, rack_count * slot_count
        )
        half_rows = lax.dynamic_slice_in_dim(outgoing, half_index * half_width, half_width, 2)
        slot_rows = lax.all_to_all(half_rows, "rack", split_axis=0, concat_axis=0, tiled=True)
        layout = slot_rows.shape
        flat_rows = slot_rows.reshape(-1, half_width)
        gate_up = jnp.dot(flat_rows, gate_up_weight, preferred_element_type=jnp.float32)
        gate_up = gate_up + swapped(gate_up.astype(jnp.bfloat16), "expert", 0).astype(gate_up.dtype)
        activated = (jax.nn.silu(gate_up[:, :part_width]) * gate_up[:, part_width:]).astype(
            jnp.bfloat16
        )
        partial_value = jnp.dot(activated, down_weight, preferred_element_type=jnp.float32).astype(
            jnp.bfloat16
        )
        partial_value = partial_value.reshape(layout)
        finished = lax.all_to_all(partial_value, "rack", split_axis=0, concat_axis=0, tiled=True)
        partial_sum = jnp.dot(
            combine_map, finished.reshape(-1, half_width), preferred_element_type=jnp.float32
        )
        full_sum = jnp.zeros((rack_rows, model_width), jnp.float32)
        full_sum = lax.dynamic_update_slice_in_dim(
            full_sum, partial_sum, half_index * half_width, 1
        )
        update = lax.psum_scatter(
            full_sum.astype(jnp.bfloat16), "expert", scatter_dimension=0, tiled=True
        ).astype(jnp.float32)
        residual = residual + update
    return residual


def solution(mesh):
    in_specs = (
        P(("rack", "expert"), None),
        P(),
        P(None, ("rack", "expert"), None),
        P(None, ("rack", "expert"), None),
        P("rack", "expert", None, None, None),
        P("rack", "expert", None, None),
    )
    out_specs = P(("rack", "expert"), None)
    dense = mesh.shape["rack"] <= TOP
    return jax.shard_map(
        dense_steps if dense else per_device, mesh=mesh, in_specs=in_specs, out_specs=out_specs, check_vma=False
    )
```

```python
import functools

import jax
import jax.numpy as jnp
from jax import lax
from jax.experimental import pallas as pl
from jax.experimental.pallas import tpu as pltpu
from jax.sharding import PartitionSpec as P

TOP = 8
STEPS = 4


def swapped(shard, axis, bit):
    return lax.ppermute(shard, axis, [(i, i ^ 1 << bit) for i in range(lax.axis_size(axis))])


def exchanged(shard, axis, mask):
    return lax.ppermute(shard, axis, [(i, i ^ mask) for i in range(lax.axis_size(axis))])


def widened(values):
    return values.astype(jnp.float32)


def rounded(values):
    return values.astype(jnp.bfloat16)


def exchanged_both(shard, rack_mask, expert_mask):
    groups = lax.axis_size("expert")
    pairs = [
        (rack * groups + group, (rack ^ rack_mask) * groups + (group ^ expert_mask))
        for rack in range(lax.axis_size("rack"))
        for group in range(groups)
    ]
    return lax.ppermute(shard, ("rack", "expert"), pairs)


def crossed(rack_mask, expert_mask):
    changed = bin(rack_mask >> 1).count("1") + bin(expert_mask >> 1).count("1")
    return rack_mask ^ changed % 2, expert_mask


def gather_masks(rack_count, group_count):
    near = [(0, 0), (2, 0), (1, 1), (3, 1)]
    far = [crossed(rack, group) for group in range(0, group_count, 2) for rack in range(0, rack_count, 4)]
    return near, far


WHOLE = pl.BlockSpec(memory_space=pltpu.VMEM)
IN_HBM = pl.BlockSpec(memory_space=pltpu.HBM)
LANES = 128
PIECES = 2


def in_vmem(shape, dtype):
    return pltpu.VMEM(shape, dtype)


def kernel_call(body, out_shape, operands, flops=0, in_hbm=(), scratch=(), limit=4):
    operands = [pltpu.with_memory_space_constraint(o, pltpu.VMEM) for o in operands]
    in_hbm = [pltpu.with_memory_space_constraint(o, pltpu.HBM) for o in in_hbm]
    read = sum(o.size * o.dtype.itemsize for o in [*operands, *in_hbm])
    return pl.pallas_call(
        body,
        out_shape=out_shape,
        in_specs=[WHOLE] * len(operands) + [IN_HBM] * len(in_hbm),
        out_specs=[WHOLE] * len(out_shape),
        scratch_shapes=scratch,
        compiler_params=pltpu.CompilerParams(vmem_limit_bytes=limit * 2**20),
        cost_estimate=pl.CostEstimate(flops=flops, bytes_accessed=read, transcendentals=0),
    )(*operands, *in_hbm)


def column_blocks(width):
    block = next(b for b in (512, 256, 128, width) if width % b == 0)
    return [slice(start, start + block) for start in range(0, width, block)]


def row_blocks(values, start, stop):
    return [values[:, at : at + LANES] for at in range(start, stop, LANES)]


def message_body(hidden_in, ids_in, levels_in, gain_in, own_ref, other_ref, gain_ref, hidden, ids, levels, gain, semaphores):
    copies = [
        pltpu.make_async_copy(source, target, semaphores.at[k])
        for k, (source, target) in enumerate(
            [(hidden_in, hidden), (ids_in, ids), (levels_in, levels), (gain_in, gain)]
        )
    ]
    for copy in copies:
        copy.start()
    for copy in copies:
        copy.wait()
    half_width = hidden.shape[1] // 2
    half_rows = half_width // LANES
    is_first = lax.axis_index("expert") % 2 == 0
    row = lax.broadcasted_iota(jnp.int32, own_ref.shape, 0)

    def route_row(ref):
        values = [widened(ref[step]) for step in range(ref.shape[0])]
        used = len(values) * values[0].shape[1]
        return jnp.concatenate(values + [jnp.zeros((1, LANES - used), jnp.float32)], axis=1)

    routing = [route_row(ids), route_row(levels)]
    features = widened(hidden[...])
    first = row_blocks(features, 0, half_width)
    second = row_blocks(features, half_width, 2 * half_width)
    for target, pairs in ((own_ref, zip(first, second)), (other_ref, zip(second, first))):
        message = jnp.zeros(own_ref.shape, jnp.float32)
        for place, values in enumerate([jnp.where(is_first, a, b) for a, b in pairs] + routing):
            message = jnp.where(row == place, values, message)
        target[...] = rounded(message)
    for place in range(half_rows):
        gain_ref[:, place * LANES : (place + 1) * LANES] = jnp.where(
            is_first, gain[place : place + 1], gain[half_rows + place : half_rows + place + 1]
        )


def weights_body(*refs, first, before):
    gate_up_ref, weight_ref, arrived_ref, semaphores = refs[before:]
    part = arrived_ref.shape[2]
    count = semaphores.shape[0]
    block = arrived_ref.shape[0] // count
    blocks = [pl.ds(k * block, block) for k in range(count)]
    copies = [
        pltpu.make_async_copy(
            gate_up_ref.at[pl.ds(first + k * block, block)], arrived_ref.at[rows], semaphores.at[k]
        )
        for k, rows in enumerate(blocks)
    ]
    for copy in copies:
        copy.start()
    for copy, rows in zip(copies, blocks):
        copy.wait()
        weight_ref[rows] = arrived_ref[rows].reshape(block, 2 * part)


def joined_body(piece_count, *refs):
    pieces, out_ref = refs[:piece_count], refs[-1]
    size = out_ref.shape[0] // len(pieces)
    for k, piece in enumerate(pieces):
        out_ref[k * size : (k + 1) * size] = piece[...].reshape(size, *out_ref.shape[1:])


def own_core_of():
    rack, group = lax.axis_index("rack"), lax.axis_index("expert") // 2
    bits = [rack // 2**k for k in range(lax.axis_size("rack").bit_length() - 1)]
    bits += [group // 2**k for k in range(lax.axis_size("expert").bit_length() - 2)]
    return sum(bits) % 2


def own_place_of(core_rows, group_count):
    rack = lax.axis_index("rack")
    return (rack + own_core_of()) % 2 * core_rows + rack // 2 * group_count + lax.axis_index("expert")


def placed(gathered_refs, half_width, rack_count, group_count):
    wide = jnp.concatenate([ref[...].reshape(ref.shape[0], -1) for ref in gathered_refs], axis=0)
    count = wide.shape[0]
    place = lax.broadcasted_iota(jnp.int32, (count, count), 0)
    source = lax.broadcasted_iota(jnp.int32, (count, count), 1)
    near, far = gather_masks(rack_count, group_count)
    distance = source // (count // 2) * (count // 2)
    for masks, index in ((near, source % len(near)), (far, source // len(near) % len(far))):
        for k, (rack, group) in enumerate(masks):
            step = rack % 2 * (count // 2) + rack // 2 * group_count + group
            distance = distance ^ jnp.where(index == k, step, 0)
    own_place = own_place_of(count // 2, group_count)
    to_place = rounded(jnp.where(place == (distance ^ own_place), 1.0, 0.0))
    wide = jnp.dot(to_place, wide, preferred_element_type=jnp.float32)
    residual = wide[:, :half_width]
    ids = wide[:, half_width : half_width + LANES]
    levels = wide[:, half_width + LANES : half_width + 2 * LANES]
    lane = lax.broadcasted_iota(jnp.int32, ids.shape, 1)
    chosen = ids == lax.axis_index("rack").astype(jnp.float32)
    mixing = jnp.zeros(ids.shape, jnp.float32)
    for step in range(STEPS):
        of_step = lane // TOP == step
        total = jnp.sum(jnp.where(of_step, levels, 0.0), axis=1, keepdims=True)
        share = jnp.sum(jnp.where(of_step & chosen, levels / total, 0.0), axis=1, keepdims=True)
        mixing = jnp.where(lane == step, widened(rounded(share)), mixing)
    return residual, mixing


def piece_columns(piece, part):
    size = part // PIECES
    return [slice(start, start + size) for start in (piece * size, part + piece * size)]


def multiplied(scaled, upper_ref, lower_ref, piece, product_ref, message_ref):
    depth, width = upper_ref.shape
    size = width // 2 // PIECES
    for k, columns in enumerate(piece_columns(piece, width // 2)):
        product = jnp.dot(scaled[:, :depth], upper_ref[:, columns], preferred_element_type=jnp.float32)
        product += jnp.dot(scaled[:, depth:], lower_ref[:, columns], preferred_element_type=jnp.float32)
        product_ref[:, k * size : (k + 1) * size] = product
        message_ref[:, k * size : (k + 1) * size] = rounded(product)


def first_piece_body(step, rack_count, group_count, *refs):
    first, last = step == 0, step == STEPS - 1
    if first:
        *gathered_refs, gain_ref, upper_ref, lower_ref, residual_ref, mixing_ref, scaled_ref, product_ref, message_ref = refs
        residual, mixing_ref[...] = placed(gathered_refs, gain_ref.shape[1], rack_count, group_count)
        residual_ref[...] = residual
    else:
        before_ref, own_ref, other_ref, gain_ref, upper_ref, lower_ref, *residual_refs, scaled_ref, product_ref, message_ref = refs
        residual = before_ref[...] + jnp.concatenate([own_ref[...], widened(other_ref[...])], axis=0)
        if last:
            place = lax.broadcasted_iota(jnp.int32, (residual.shape[0], 1), 0)
            own_place = own_place_of(residual.shape[0] // 2, group_count)
            for ref, wanted in zip(residual_refs, (own_place, own_place ^ 1)):
                ref[...] = jnp.sum(jnp.where(place == wanted, residual, 0.0), axis=0, keepdims=True)
        else:
            residual_refs[0][...] = residual
    scaled = rounded(residual * gain_ref[...])
    scaled_ref[...] = scaled
    multiplied(scaled, upper_ref, lower_ref, 0, product_ref, message_ref)
    square_sum = jnp.sum(residual * residual, axis=1, keepdims=True)
    square_high = widened(rounded(square_sum))
    lane = lax.broadcasted_iota(jnp.int32, (residual.shape[0], LANES), 1)
    tail = jnp.where(lane == 0, square_high, square_sum - square_high)
    message_ref[:, product_ref.shape[1] :] = rounded(tail)


def other_piece_body(piece, scaled_ref, upper_ref, lower_ref, product_ref, message_ref):
    multiplied(scaled_ref[...], upper_ref, lower_ref, piece, product_ref, message_ref)


def down_body(step, piece, model_width, group_count, tail_ref, other_tail_ref, product_ref, swapped_ref, mixing_ref, weight_ref, *refs):
    width = product_ref.shape[1]
    size = width // 2
    tails = widened(tail_ref[:, width:]) + widened(other_tail_ref[:, width:])
    square_sum = tails[:, 0:1] + tails[:, 1:2]
    scale = lax.rsqrt(square_sum / model_width + 1e-06)
    whole = product_ref[...] + widened(swapped_ref[:, :width])
    gate = whole[:, :size] * scale
    up = whole[:, size:] * scale
    activated = rounded(gate / (1.0 + jnp.exp(-gate)) * up)
    mixing = mixing_ref[...]
    count = mixing.shape[0]
    last = step == STEPS - 1
    mixing = mixing[:, step : step + 1]
    rows = slice(piece * size, (piece + 1) * size)
    before_refs, out_refs = (refs[:1], refs[1:]) if piece else ((), refs)
    final = piece == PIECES - 1
    for columns in [slice(0, weight_ref.shape[1])] if last and final else column_blocks(weight_ref.shape[1]):
        term = jnp.dot(activated, weight_ref[rows, columns], preferred_element_type=jnp.float32)
        for ref in before_refs:
            term = term + ref[:, columns]
        if not final:
            out_refs[0][:, columns] = term
            continue
        update = widened(rounded(term)) * mixing
        if not last:
            out_refs[0][:, columns] = update[: count // 2]
            out_refs[1][:, columns] = rounded(update[count // 2 :])
            continue
        blocks = rounded(update).reshape(count, -1, LANES)
        for start in range(0, count, group_count):
            chip, core = start % (count // 2) // group_count, (start // (count // 2) + own_core_of()) % 2
            out_refs[0][pl.ds((2 * chip + core) * group_count, group_count)] = blocks[start : start + group_count]


def result_body(arrived_ref, own_ref, other_ref, out_ref):
    count, half_width = arrived_ref.shape[0], own_ref.shape[1]
    terms = widened(arrived_ref[...].reshape(count, half_width))
    of_first = lax.broadcasted_iota(jnp.int32, (count, 1), 0) % 2 == 0
    is_first = lax.axis_index("expert") % 2 == 0
    own, other = own_ref[...], other_ref[...]
    out_ref[:, :half_width] = jnp.where(is_first, own, other) + jnp.sum(
        jnp.where(of_first, terms, 0.0), axis=0, keepdims=True
    )
    out_ref[:, half_width:] = jnp.where(is_first, other, own) + jnp.sum(
        jnp.where(of_first, 0.0, terms), axis=0, keepdims=True
    )


def dense_steps(hidden_in, norm_gain, expert_ids, gate_levels, w_gate_up, w_down):
    rack_count = lax.axis_size("rack")
    group_count = lax.axis_size("expert")
    core_rows = rack_count // 2 * group_count
    token_count = 2 * core_rows
    model_width = hidden_in.shape[1]
    half_width = model_width // 2
    part_width = w_down.shape[2]
    product_width = 2 * part_width
    product_flops = 2 * token_count * half_width * product_width

    block_shape = (half_width // LANES + 2, LANES)
    sources = [hidden_in, expert_ids, gate_levels, norm_gain.reshape(-1, LANES)]
    own, other, gain_half = kernel_call(
        message_body,
        [
            in_vmem(block_shape, jnp.bfloat16),
            in_vmem(block_shape, jnp.bfloat16),
            in_vmem((1, half_width), jnp.float32),
        ],
        [],
        in_hbm=sources,
        scratch=[*(in_vmem(a.shape, a.dtype) for a in sources), pltpu.SemaphoreType.DMA((len(sources),))],
    )
    block = next(b for b in (128, 16, half_width) if half_width % b == 0)

    def turned(start, stop, *before):
        return kernel_call(
            functools.partial(weights_body, first=start, before=len(before)),
            [in_vmem((stop - start, product_width), jnp.bfloat16)],
            before,
            in_hbm=[w_gate_up[0, 0]],
            scratch=[
                in_vmem((stop - start, 2, part_width), jnp.bfloat16),
                pltpu.SemaphoreType.DMA(((stop - start) // block,)),
            ],
            limit=12,
        )[0]

    def joined(pieces, count, *before):
        out_shape = [in_vmem((count,) + block_shape, jnp.bfloat16)]
        return kernel_call(functools.partial(joined_body, len(pieces)), out_shape, [*pieces, *before])[0]

    near, far = gather_masks(rack_count, group_count)
    middle = -(-half_width // 2 // 256) * 256
    upper = turned(0, middle)
    rows = [own] + [exchanged_both(other if group else own, rack, group) for rack, group in near[1:]]
    rows = joined(rows, len(near), upper)
    lower = turned(middle, half_width, rows)
    gate_up_weights = [upper, lower]
    rows = [rows] + [exchanged_both(rows, rack, group) for rack, group in far[1:]]
    rows = joined(rows, core_rows, lower)
    gathered = [rows, exchanged(rows, "rack", 1)]

    piece_width = product_width // PIECES
    for step_index in range(STEPS):
        last = step_index == STEPS - 1
        product_shape = in_vmem((token_count, piece_width), jnp.float32)
        kept = [in_vmem((token_count, half_width), jnp.float32)]
        if step_index == 0:
            operands = gathered
            kept += [in_vmem((token_count, LANES), jnp.float32)]
        else:
            operands = [residual, update, received]
        if last:
            kept = [in_vmem((1, half_width), jnp.float32)] * 2
        *kept, scaled, product, message = kernel_call(
            functools.partial(first_piece_body, step_index, rack_count, group_count),
            [
                *kept,
                in_vmem((token_count, half_width), jnp.bfloat16),
                product_shape,
                in_vmem((token_count, piece_width + LANES), jnp.bfloat16),
            ],
            operands + [gain_half, *gate_up_weights],
            product_flops // PIECES,
        )
        if step_index == 0:
            residual, mixing = kept
        else:
            residual = kept[0]
        products, swapped = [product], [exchanged(message, "expert", 1)]
        for piece in range(1, PIECES):
            product, piece_message = kernel_call(
                functools.partial(other_piece_body, piece),
                [product_shape, in_vmem((token_count, piece_width), jnp.bfloat16)],
                [scaled, *gate_up_weights],
                product_flops // PIECES,
            )
            products.append(product)
            swapped.append(exchanged(piece_message, "expert", 1))
        if last:
            own_row, other_row = kept
            other_row = exchanged(other_row, "expert", 1)
        updates = []
        for piece in range(PIECES):
            if piece < PIECES - 1:
                shapes = [in_vmem((token_count, half_width), jnp.float32)]
            elif last:
                shapes = [in_vmem((token_count, half_width // LANES, LANES), jnp.bfloat16)]
            else:
                shapes = [
                    in_vmem((core_rows, half_width), jnp.float32),
                    in_vmem((core_rows, half_width), jnp.bfloat16),
                ]
            updates = kernel_call(
                functools.partial(down_body, step_index, piece, model_width, group_count),
                shapes,
                [message, swapped[0], products[piece], swapped[piece], mixing, w_down[0, 0], *updates],
                product_flops // 2 // PIECES,
            )
        if last:
            updates = lax.optimization_barrier((updates[0], other_row))
            break
        update = updates[0] + widened(exchanged(updates[1], "rack", 1))
        sent = rounded(update)
        for mask in range(2, rack_count, 2):
            update = update + widened(exchanged_both(sent, *crossed(mask, 0)))
        sent = rounded(update)
        for mask in range(2, group_count, 2):
            update = update + widened(exchanged_both(sent, *crossed(0, mask)))
        received = exchanged(rounded(update), "rack", 1)

    arrived = lax.all_to_all(updates[0], ("rack", "expert"), split_axis=0, concat_axis=0, tiled=True)
    (result,) = kernel_call(
        result_body, [jax.ShapeDtypeStruct((1, model_width), jnp.float32)], [arrived, own_row, updates[1]]
    )
    return result


def per_device(hidden_in, norm_gain, expert_ids, gate_levels, w_gate_up, w_down):
    rack_count = lax.axis_size("rack")
    group_count = lax.axis_size("expert")
    group_index = lax.axis_index("expert")
    half_index = group_index % 2
    tok_rows = hidden_in.shape[0]
    rack_rows = tok_rows * group_count
    slot_count = min(rack_rows, 3 * rack_rows * TOP // (2 * rack_count))
    model_width = hidden_in.shape[1]
    half_width = model_width // 2
    part_width = w_down.shape[2]
    gate_up_weight = w_gate_up[0, 0].reshape(half_width, 2 * part_width)
    down_weight = w_down[0, 0]
    all_ids, all_levels = (
        lax.all_gather(expert_ids, "expert", axis=1, tiled=True),
        lax.all_gather(gate_levels, "expert", axis=1, tiled=True),
    )
    expert_range = jnp.arange(rack_count, dtype=jnp.int32)
    slot_ids = jnp.arange(slot_count, dtype=jnp.int32)
    residual = hidden_in.astype(jnp.float32)
    for step_index in range(STEPS):
        mean_square = jnp.mean(residual * residual, axis=-1, keepdims=True)
        normed = (residual * lax.rsqrt(mean_square + 1e-06) * norm_gain).astype(jnp.bfloat16)
        rack_normed = lax.all_gather(normed, "expert", axis=0, tiled=True)
        picked = all_ids[step_index]
        level_vals = all_levels[step_index].astype(jnp.float32)
        shares = level_vals / jnp.sum(level_vals, axis=-1, keepdims=True)
        matches = picked[:, :, None] == expert_range[None, None, :]
        chosen = jnp.sum(matches.astype(jnp.int32), axis=1)
        mixing = jnp.sum(jnp.where(matches, shares[:, :, None], jnp.float32(0.0)), axis=1).astype(
            jnp.bfloat16
        )
        slot_rank = jnp.cumsum(chosen, axis=0) - chosen
        placement = chosen[:, :, None] * (slot_rank[:, :, None] == slot_ids).astype(jnp.int32)
        dispatch_map = (
            jnp.transpose(placement, (1, 2, 0))
            .reshape(rack_count * slot_count, rack_rows)
            .astype(jnp.bfloat16)
        )
        outgoing = jnp.dot(dispatch_map, rack_normed, preferred_element_type=jnp.float32).astype(
            jnp.bfloat16
        )
        outgoing = outgoing.reshape(rack_count, slot_count, model_width)
        combine_map = (placement.astype(jnp.bfloat16) * mixing[:, :, None]).reshape(
            rack_rows, rack_count * slot_count
        )
        half_rows = lax.dynamic_slice_in_dim(outgoing, half_index * half_width, half_width, 2)
        slot_rows = lax.all_to_all(half_rows, "rack", split_axis=0, concat_axis=0, tiled=True)
        layout = slot_rows.shape
        flat_rows = slot_rows.reshape(-1, half_width)
        gate_up = jnp.dot(flat_rows, gate_up_weight, preferred_element_type=jnp.float32)
        gate_up = gate_up + swapped(gate_up.astype(jnp.bfloat16), "expert", 0).astype(gate_up.dtype)
        activated = (jax.nn.silu(gate_up[:, :part_width]) * gate_up[:, part_width:]).astype(
            jnp.bfloat16
        )
        partial_value = jnp.dot(activated, down_weight, preferred_element_type=jnp.float32).astype(
            jnp.bfloat16
        )
        partial_value = partial_value.reshape(layout)
        finished = lax.all_to_all(partial_value, "rack", split_axis=0, concat_axis=0, tiled=True)
        partial_sum = jnp.dot(
            combine_map, finished.reshape(-1, half_width), preferred_element_type=jnp.float32
        )
        full_sum = jnp.zeros((rack_rows, model_width), jnp.float32)
        full_sum = lax.dynamic_update_slice_in_dim(
            full_sum, partial_sum, half_index * half_width, 1
        )
        update = lax.psum_scatter(
            full_sum.astype(jnp.bfloat16), "expert", scatter_dimension=0, tiled=True
        ).astype(jnp.float32)
        residual = residual + update
    return residual


def solution(mesh):
    in_specs = (
        P(("rack", "expert"), None),
        P(),
        P(None, ("rack", "expert"), None),
        P(None, ("rack", "expert"), None),
        P("rack", "expert", None, None, None),
        P("rack", "expert", None, None),
    )
    out_specs = P(("rack", "expert"), None)
    dense = mesh.shape["rack"] <= TOP
    return jax.shard_map(
        dense_steps if dense else per_device, mesh=mesh, in_specs=in_specs, out_specs=out_specs, check_vma=False
    )
```

```python
import functools

import jax
import jax.numpy as jnp
from jax import lax
from jax.experimental import pallas as pl
from jax.experimental.pallas import tpu as pltpu
from jax.sharding import PartitionSpec as P

TOP = 8
STEPS = 4


def swapped(shard, axis, bit):
    return lax.ppermute(shard, axis, [(i, i ^ 1 << bit) for i in range(lax.axis_size(axis))])


def exchanged(shard, axis, mask):
    return lax.ppermute(shard, axis, [(i, i ^ mask) for i in range(lax.axis_size(axis))])


def widened(values):
    return values.astype(jnp.float32)


def rounded(values):
    return values.astype(jnp.bfloat16)


def exchanged_both(shard, rack_mask, expert_mask):
    groups = lax.axis_size("expert")
    pairs = [
        (rack * groups + group, (rack ^ rack_mask) * groups + (group ^ expert_mask))
        for rack in range(lax.axis_size("rack"))
        for group in range(groups)
    ]
    return lax.ppermute(shard, ("rack", "expert"), pairs)


def crossed(rack_mask, expert_mask):
    changed = bin(rack_mask >> 1).count("1") + bin(expert_mask >> 1).count("1")
    return rack_mask ^ changed % 2, expert_mask


def gather_masks(rack_count, group_count):
    near = [(0, 0), (3, 0), (1, 1), (2, 1)]
    far = [crossed(rack, group) for group in range(0, group_count, 2) for rack in range(0, rack_count, 4)]
    return near, far


WHOLE = pl.BlockSpec(memory_space=pltpu.VMEM)
IN_HBM = pl.BlockSpec(memory_space=pltpu.HBM)
LANES = 128
PIECES = 2


def in_vmem(shape, dtype):
    return pltpu.VMEM(shape, dtype)


def kernel_call(body, out_shape, operands, flops=0, in_hbm=(), scratch=(), limit=4):
    operands = [pltpu.with_memory_space_constraint(o, pltpu.VMEM) for o in operands]
    in_hbm = [pltpu.with_memory_space_constraint(o, pltpu.HBM) for o in in_hbm]
    read = sum(o.size * o.dtype.itemsize for o in [*operands, *in_hbm])
    return pl.pallas_call(
        body,
        out_shape=out_shape,
        in_specs=[WHOLE] * len(operands) + [IN_HBM] * len(in_hbm),
        out_specs=[WHOLE] * len(out_shape),
        scratch_shapes=scratch,
        compiler_params=pltpu.CompilerParams(vmem_limit_bytes=limit * 2**20),
        cost_estimate=pl.CostEstimate(flops=flops, bytes_accessed=read, transcendentals=0),
    )(*operands, *in_hbm)


def column_blocks(width):
    block = next(b for b in (512, 256, 128, width) if width % b == 0)
    return [slice(start, start + block) for start in range(0, width, block)]


def row_blocks(values, start, stop):
    return [values[:, at : at + LANES] for at in range(start, stop, LANES)]


def message_body(hidden_in, ids_in, levels_in, gain_in, own_ref, other_ref, gain_ref, hidden, ids, levels, gain, semaphores):
    copies = [
        pltpu.make_async_copy(source, target, semaphores.at[k])
        for k, (source, target) in enumerate(
            [(hidden_in, hidden), (ids_in, ids), (levels_in, levels), (gain_in, gain)]
        )
    ]
    for copy in copies:
        copy.start()
    for copy in copies:
        copy.wait()
    half_width = hidden.shape[1] // 2
    half_rows = half_width // LANES
    is_first = lax.axis_index("expert") % 2 == 0
    row = lax.broadcasted_iota(jnp.int32, own_ref.shape, 0)

    def route_row(ref):
        values = [widened(ref[step]) for step in range(ref.shape[0])]
        used = len(values) * values[0].shape[1]
        return jnp.concatenate(values + [jnp.zeros((1, LANES - used), jnp.float32)], axis=1)

    routing = [route_row(ids), route_row(levels)]
    features = widened(hidden[...])
    first = row_blocks(features, 0, half_width)
    second = row_blocks(features, half_width, 2 * half_width)
    for target, pairs in ((own_ref, zip(first, second)), (other_ref, zip(second, first))):
        message = jnp.zeros(own_ref.shape, jnp.float32)
        for place, values in enumerate([jnp.where(is_first, a, b) for a, b in pairs] + routing):
            message = jnp.where(row == place, values, message)
        target[...] = rounded(message)
    for place in range(half_rows):
        gain_ref[:, place * LANES : (place + 1) * LANES] = jnp.where(
            is_first, gain[place : place + 1], gain[half_rows + place : half_rows + place + 1]
        )


def weights_body(*refs, first, before):
    gate_up_ref, weight_ref, arrived_ref, semaphores = refs[before:]
    part = arrived_ref.shape[2]
    count = semaphores.shape[0]
    block = arrived_ref.shape[0] // count
    blocks = [pl.ds(k * block, block) for k in range(count)]
    copies = [
        pltpu.make_async_copy(
            gate_up_ref.at[pl.ds(first + k * block, block)], arrived_ref.at[rows], semaphores.at[k]
        )
        for k, rows in enumerate(blocks)
    ]
    for copy in copies:
        copy.start()
    for copy, rows in zip(copies, blocks):
        copy.wait()
        weight_ref[rows] = arrived_ref[rows].reshape(block, 2 * part)


def joined_body(piece_count, *refs):
    pieces, out_ref = refs[:piece_count], refs[-1]
    size = out_ref.shape[0] // len(pieces)
    for k, piece in enumerate(pieces):
        out_ref[k * size : (k + 1) * size] = piece[...].reshape(size, *out_ref.shape[1:])


def own_core_of():
    rack, group = lax.axis_index("rack"), lax.axis_index("expert") // 2
    bits = [rack // 2**k for k in range(lax.axis_size("rack").bit_length() - 1)]
    bits += [group // 2**k for k in range(lax.axis_size("expert").bit_length() - 2)]
    return sum(bits) % 2


def own_place_of(core_rows, group_count):
    rack = lax.axis_index("rack")
    return (rack + own_core_of()) % 2 * core_rows + rack // 2 * group_count + lax.axis_index("expert")


def placed(gathered_refs, half_width, rack_count, group_count):
    wide = jnp.concatenate([ref[...].reshape(ref.shape[0], -1) for ref in gathered_refs], axis=0)
    count = wide.shape[0]
    place = lax.broadcasted_iota(jnp.int32, (count, count), 0)
    source = lax.broadcasted_iota(jnp.int32, (count, count), 1)
    near, far = gather_masks(rack_count, group_count)
    distance = source // (count // 2) * (count // 2)
    for masks, index in ((near, source % len(near)), (far, source // len(near) % len(far))):
        for k, (rack, group) in enumerate(masks):
            step = rack % 2 * (count // 2) + rack // 2 * group_count + group
            distance = distance ^ jnp.where(index == k, step, 0)
    own_place = own_place_of(count // 2, group_count)
    to_place = rounded(jnp.where(place == (distance ^ own_place), 1.0, 0.0))
    wide = jnp.dot(to_place, wide, preferred_element_type=jnp.float32)
    residual = wide[:, :half_width]
    ids = wide[:, half_width : half_width + LANES]
    levels = wide[:, half_width + LANES : half_width + 2 * LANES]
    lane = lax.broadcasted_iota(jnp.int32, ids.shape, 1)
    chosen = ids == lax.axis_index("rack").astype(jnp.float32)
    mixing = jnp.zeros(ids.shape, jnp.float32)
    for step in range(STEPS):
        of_step = lane // TOP == step
        total = jnp.sum(jnp.where(of_step, levels, 0.0), axis=1, keepdims=True)
        share = jnp.sum(jnp.where(of_step & chosen, levels / total, 0.0), axis=1, keepdims=True)
        mixing = jnp.where(lane == step, widened(rounded(share)), mixing)
    return residual, mixing


def piece_columns(piece, part):
    size = part // PIECES
    return [slice(start, start + size) for start in (piece * size, part + piece * size)]


def multiplied(scaled, upper_ref, lower_ref, piece, product_ref, message_ref):
    depth, width = upper_ref.shape
    size = width // 2 // PIECES
    for k, columns in enumerate(piece_columns(piece, width // 2)):
        product = jnp.dot(scaled[:, :depth], upper_ref[:, columns], preferred_element_type=jnp.float32)
        product += jnp.dot(scaled[:, depth:], lower_ref[:, columns], preferred_element_type=jnp.float32)
        product_ref[:, k * size : (k + 1) * size] = product
        message_ref[:, k * size : (k + 1) * size] = rounded(product)


def first_piece_body(step, rack_count, group_count, *refs):
    first, last = step == 0, step == STEPS - 1
    if first:
        *gathered_refs, gain_ref, upper_ref, lower_ref, residual_ref, mixing_ref, scaled_ref, product_ref, message_ref = refs
        residual, mixing_ref[...] = placed(gathered_refs, gain_ref.shape[1], rack_count, group_count)
        residual_ref[...] = residual
    else:
        before_ref, own_ref, other_ref, gain_ref, upper_ref, lower_ref, *residual_refs, scaled_ref, product_ref, message_ref = refs
        residual = before_ref[...] + jnp.concatenate([own_ref[...], widened(other_ref[...])], axis=0)
        if last:
            place = lax.broadcasted_iota(jnp.int32, (residual.shape[0], 1), 0)
            own_place = own_place_of(residual.shape[0] // 2, group_count)
            for ref, wanted in zip(residual_refs, (own_place, own_place ^ 1)):
                ref[...] = jnp.sum(jnp.where(place == wanted, residual, 0.0), axis=0, keepdims=True)
        else:
            residual_refs[0][...] = residual
    scaled = rounded(residual * gain_ref[...])
    scaled_ref[...] = scaled
    multiplied(scaled, upper_ref, lower_ref, 0, product_ref, message_ref)
    square_sum = jnp.sum(residual * residual, axis=1, keepdims=True)
    square_high = widened(rounded(square_sum))
    lane = lax.broadcasted_iota(jnp.int32, (residual.shape[0], LANES), 1)
    tail = jnp.where(lane == 0, square_high, square_sum - square_high)
    message_ref[:, product_ref.shape[1] :] = rounded(tail)


def other_piece_body(piece, scaled_ref, upper_ref, lower_ref, product_ref, message_ref):
    multiplied(scaled_ref[...], upper_ref, lower_ref, piece, product_ref, message_ref)


def down_body(step, piece, model_width, group_count, tail_ref, other_tail_ref, product_ref, swapped_ref, mixing_ref, weight_ref, *refs):
    width = product_ref.shape[1]
    size = width // 2
    tails = widened(tail_ref[:, width:]) + widened(other_tail_ref[:, width:])
    square_sum = tails[:, 0:1] + tails[:, 1:2]
    scale = lax.rsqrt(square_sum / model_width + 1e-06)
    whole = product_ref[...] + widened(swapped_ref[:, :width])
    gate = whole[:, :size] * scale
    up = whole[:, size:] * scale
    activated = rounded(gate / (1.0 + jnp.exp(-gate)) * up)
    mixing = mixing_ref[...]
    count = mixing.shape[0]
    last = step == STEPS - 1
    mixing = mixing[:, step : step + 1]
    rows = slice(piece * size, (piece + 1) * size)
    before_refs, out_refs = (refs[:1], refs[1:]) if piece else ((), refs)
    final = piece == PIECES - 1
    for columns in [slice(0, weight_ref.shape[1])] if last and final else column_blocks(weight_ref.shape[1]):
        term = jnp.dot(activated, weight_ref[rows, columns], preferred_element_type=jnp.float32)
        for ref in before_refs:
            term = term + ref[:, columns]
        if not final:
            out_refs[0][:, columns] = term
            continue
        update = widened(rounded(term)) * mixing
        if not last:
            out_refs[0][:, columns] = update[: count // 2]
            out_refs[1][:, columns] = rounded(update[count // 2 :])
            continue
        blocks = rounded(update).reshape(count, -1, LANES)
        for start in range(0, count, group_count):
            chip, core = start % (count // 2) // group_count, (start // (count // 2) + own_core_of()) % 2
            out_refs[0][pl.ds((2 * chip + core) * group_count, group_count)] = blocks[start : start + group_count]


def result_body(arrived_ref, own_ref, other_ref, out_ref):
    count, half_width = arrived_ref.shape[0], own_ref.shape[1]
    terms = widened(arrived_ref[...].reshape(count, half_width))
    of_first = lax.broadcasted_iota(jnp.int32, (count, 1), 0) % 2 == 0
    is_first = lax.axis_index("expert") % 2 == 0
    own, other = own_ref[...], other_ref[...]
    out_ref[:, :half_width] = jnp.where(is_first, own, other) + jnp.sum(
        jnp.where(of_first, terms, 0.0), axis=0, keepdims=True
    )
    out_ref[:, half_width:] = jnp.where(is_first, other, own) + jnp.sum(
        jnp.where(of_first, 0.0, terms), axis=0, keepdims=True
    )


def dense_steps(hidden_in, norm_gain, expert_ids, gate_levels, w_gate_up, w_down):
    rack_count = lax.axis_size("rack")
    group_count = lax.axis_size("expert")
    core_rows = rack_count // 2 * group_count
    token_count = 2 * core_rows
    model_width = hidden_in.shape[1]
    half_width = model_width // 2
    part_width = w_down.shape[2]
    product_width = 2 * part_width
    product_flops = 2 * token_count * half_width * product_width

    block_shape = (half_width // LANES + 2, LANES)
    sources = [hidden_in, expert_ids, gate_levels, norm_gain.reshape(-1, LANES)]
    own, other, gain_half = kernel_call(
        message_body,
        [
            in_vmem(block_shape, jnp.bfloat16),
            in_vmem(block_shape, jnp.bfloat16),
            in_vmem((1, half_width), jnp.float32),
        ],
        [],
        in_hbm=sources,
        scratch=[*(in_vmem(a.shape, a.dtype) for a in sources), pltpu.SemaphoreType.DMA((len(sources),))],
    )
    block = next(b for b in (128, 16, half_width) if half_width % b == 0)

    def turned(start, stop, *before):
        return kernel_call(
            functools.partial(weights_body, first=start, before=len(before)),
            [in_vmem((stop - start, product_width), jnp.bfloat16)],
            before,
            in_hbm=[w_gate_up[0, 0]],
            scratch=[
                in_vmem((stop - start, 2, part_width), jnp.bfloat16),
                pltpu.SemaphoreType.DMA(((stop - start) // block,)),
            ],
            limit=12,
        )[0]

    def joined(pieces, count, *before):
        out_shape = [in_vmem((count,) + block_shape, jnp.bfloat16)]
        return kernel_call(functools.partial(joined_body, len(pieces)), out_shape, [*pieces, *before])[0]

    near, far = gather_masks(rack_count, group_count)
    middle = -(-half_width // 2 // 256) * 256
    upper = turned(0, middle)
    rows = [own] + [exchanged_both(other if group else own, rack, group) for rack, group in near[1:]]
    rows = joined(rows, len(near), upper)
    lower = turned(middle, half_width, rows)
    gate_up_weights = [upper, lower]
    rows = [rows] + [exchanged_both(rows, rack, group) for rack, group in far[1:]]
    rows = joined(rows, core_rows, lower)
    gathered = [rows, exchanged(rows, "rack", 1)]

    piece_width = product_width // PIECES
    for step_index in range(STEPS):
        last = step_index == STEPS - 1
        product_shape = in_vmem((token_count, piece_width), jnp.float32)
        kept = [in_vmem((token_count, half_width), jnp.float32)]
        if step_index == 0:
            operands = gathered
            kept += [in_vmem((token_count, LANES), jnp.float32)]
        else:
            operands = [residual, update, received]
        if last:
            kept = [in_vmem((1, half_width), jnp.float32)] * 2
        *kept, scaled, product, message = kernel_call(
            functools.partial(first_piece_body, step_index, rack_count, group_count),
            [
                *kept,
                in_vmem((token_count, half_width), jnp.bfloat16),
                product_shape,
                in_vmem((token_count, piece_width + LANES), jnp.bfloat16),
            ],
            operands + [gain_half, *gate_up_weights],
            product_flops // PIECES,
        )
        if step_index == 0:
            residual, mixing = kept
        else:
            residual = kept[0]
        products, swapped = [product], [exchanged(message, "expert", 1)]
        for piece in range(1, PIECES):
            product, piece_message = kernel_call(
                functools.partial(other_piece_body, piece),
                [product_shape, in_vmem((token_count, piece_width), jnp.bfloat16)],
                [scaled, *gate_up_weights],
                product_flops // PIECES,
            )
            products.append(product)
            swapped.append(exchanged(piece_message, "expert", 1))
        if last:
            own_row, other_row = kept
            other_row = exchanged(other_row, "expert", 1)
        updates = []
        for piece in range(PIECES):
            if piece < PIECES - 1:
                shapes = [in_vmem((token_count, half_width), jnp.float32)]
            elif last:
                shapes = [in_vmem((token_count, half_width // LANES, LANES), jnp.bfloat16)]
            else:
                shapes = [
                    in_vmem((core_rows, half_width), jnp.float32),
                    in_vmem((core_rows, half_width), jnp.bfloat16),
                ]
            updates = kernel_call(
                functools.partial(down_body, step_index, piece, model_width, group_count),
                shapes,
                [message, swapped[0], products[piece], swapped[piece], mixing, w_down[0, 0], *updates],
                product_flops // 2 // PIECES,
            )
        if last:
            updates = lax.optimization_barrier((updates[0], other_row))
            break
        update = updates[0] + widened(exchanged(updates[1], "rack", 1))
        sent = rounded(update)
        for mask in range(2, rack_count, 2):
            update = update + widened(exchanged_both(sent, *crossed(mask, 0)))
        sent = rounded(update)
        for mask in range(2, group_count, 2):
            update = update + widened(exchanged_both(sent, *crossed(0, mask)))
        received = exchanged(rounded(update), "rack", 1)

    arrived = lax.all_to_all(updates[0], ("rack", "expert"), split_axis=0, concat_axis=0, tiled=True)
    (result,) = kernel_call(
        result_body, [jax.ShapeDtypeStruct((1, model_width), jnp.float32)], [arrived, own_row, updates[1]]
    )
    return result


def per_device(hidden_in, norm_gain, expert_ids, gate_levels, w_gate_up, w_down):
    rack_count = lax.axis_size("rack")
    group_count = lax.axis_size("expert")
    group_index = lax.axis_index("expert")
    half_index = group_index % 2
    tok_rows = hidden_in.shape[0]
    rack_rows = tok_rows * group_count
    slot_count = min(rack_rows, 3 * rack_rows * TOP // (2 * rack_count))
    model_width = hidden_in.shape[1]
    half_width = model_width // 2
    part_width = w_down.shape[2]
    gate_up_weight = w_gate_up[0, 0].reshape(half_width, 2 * part_width)
    down_weight = w_down[0, 0]
    all_ids, all_levels = (
        lax.all_gather(expert_ids, "expert", axis=1, tiled=True),
        lax.all_gather(gate_levels, "expert", axis=1, tiled=True),
    )
    expert_range = jnp.arange(rack_count, dtype=jnp.int32)
    slot_ids = jnp.arange(slot_count, dtype=jnp.int32)
    residual = hidden_in.astype(jnp.float32)
    for step_index in range(STEPS):
        mean_square = jnp.mean(residual * residual, axis=-1, keepdims=True)
        normed = (residual * lax.rsqrt(mean_square + 1e-06) * norm_gain).astype(jnp.bfloat16)
        rack_normed = lax.all_gather(normed, "expert", axis=0, tiled=True)
        picked = all_ids[step_index]
        level_vals = all_levels[step_index].astype(jnp.float32)
        shares = level_vals / jnp.sum(level_vals, axis=-1, keepdims=True)
        matches = picked[:, :, None] == expert_range[None, None, :]
        chosen = jnp.sum(matches.astype(jnp.int32), axis=1)
        mixing = jnp.sum(jnp.where(matches, shares[:, :, None], jnp.float32(0.0)), axis=1).astype(
            jnp.bfloat16
        )
        slot_rank = jnp.cumsum(chosen, axis=0) - chosen
        placement = chosen[:, :, None] * (slot_rank[:, :, None] == slot_ids).astype(jnp.int32)
        dispatch_map = (
            jnp.transpose(placement, (1, 2, 0))
            .reshape(rack_count * slot_count, rack_rows)
            .astype(jnp.bfloat16)
        )
        outgoing = jnp.dot(dispatch_map, rack_normed, preferred_element_type=jnp.float32).astype(
            jnp.bfloat16
        )
        outgoing = outgoing.reshape(rack_count, slot_count, model_width)
        combine_map = (placement.astype(jnp.bfloat16) * mixing[:, :, None]).reshape(
            rack_rows, rack_count * slot_count
        )
        half_rows = lax.dynamic_slice_in_dim(outgoing, half_index * half_width, half_width, 2)
        slot_rows = lax.all_to_all(half_rows, "rack", split_axis=0, concat_axis=0, tiled=True)
        layout = slot_rows.shape
        flat_rows = slot_rows.reshape(-1, half_width)
        gate_up = jnp.dot(flat_rows, gate_up_weight, preferred_element_type=jnp.float32)
        gate_up = gate_up + swapped(gate_up.astype(jnp.bfloat16), "expert", 0).astype(gate_up.dtype)
        activated = (jax.nn.silu(gate_up[:, :part_width]) * gate_up[:, part_width:]).astype(
            jnp.bfloat16
        )
        partial_value = jnp.dot(activated, down_weight, preferred_element_type=jnp.float32).astype(
            jnp.bfloat16
        )
        partial_value = partial_value.reshape(layout)
        finished = lax.all_to_all(partial_value, "rack", split_axis=0, concat_axis=0, tiled=True)
        partial_sum = jnp.dot(
            combine_map, finished.reshape(-1, half_width), preferred_element_type=jnp.float32
        )
        full_sum = jnp.zeros((rack_rows, model_width), jnp.float32)
        full_sum = lax.dynamic_update_slice_in_dim(
            full_sum, partial_sum, half_index * half_width, 1
        )
        update = lax.psum_scatter(
            full_sum.astype(jnp.bfloat16), "expert", scatter_dimension=0, tiled=True
        ).astype(jnp.float32)
        residual = residual + update
    return residual


def solution(mesh):
    in_specs = (
        P(("rack", "expert"), None),
        P(),
        P(None, ("rack", "expert"), None),
        P(None, ("rack", "expert"), None),
        P("rack", "expert", None, None, None),
        P("rack", "expert", None, None),
    )
    out_specs = P(("rack", "expert"), None)
    dense = mesh.shape["rack"] <= TOP
    return jax.shard_map(
        dense_steps if dense else per_device, mesh=mesh, in_specs=in_specs, out_specs=out_specs, check_vma=False
    )
```

```python
import functools

import jax
import jax.numpy as jnp
from jax import lax
from jax.experimental import pallas as pl
from jax.experimental.pallas import tpu as pltpu
from jax.sharding import PartitionSpec as P

TOP = 8
STEPS = 4


def swapped(shard, axis, bit):
    return lax.ppermute(shard, axis, [(i, i ^ 1 << bit) for i in range(lax.axis_size(axis))])


def exchanged(shard, axis, mask):
    return lax.ppermute(shard, axis, [(i, i ^ mask) for i in range(lax.axis_size(axis))])


def widened(values):
    return values.astype(jnp.float32)


def rounded(values):
    return values.astype(jnp.bfloat16)


def exchanged_both(shard, rack_mask, expert_mask):
    groups = lax.axis_size("expert")
    pairs = [
        (rack * groups + group, (rack ^ rack_mask) * groups + (group ^ expert_mask))
        for rack in range(lax.axis_size("rack"))
        for group in range(groups)
    ]
    return lax.ppermute(shard, ("rack", "expert"), pairs)


def crossed(rack_mask, expert_mask):
    changed = bin(rack_mask >> 1).count("1") + bin(expert_mask >> 1).count("1")
    return rack_mask ^ changed % 2, expert_mask


def gather_masks(rack_count, group_count):
    near = [(0, 0), (3, 0), (1, 1), (2, 1)]
    far = [
        (rack ^ (group >> 1) % 2, group)
        for group in range(0, group_count, 2)
        for rack in range(0, rack_count, 4)
    ]
    return near, far


WHOLE = pl.BlockSpec(memory_space=pltpu.VMEM)
IN_HBM = pl.BlockSpec(memory_space=pltpu.HBM)
LANES = 128
PIECES = 2


def in_vmem(shape, dtype):
    return pltpu.VMEM(shape, dtype)


def kernel_call(body, out_shape, operands, flops=0, in_hbm=(), scratch=(), limit=4):
    operands = [pltpu.with_memory_space_constraint(o, pltpu.VMEM) for o in operands]
    in_hbm = [pltpu.with_memory_space_constraint(o, pltpu.HBM) for o in in_hbm]
    read = sum(o.size * o.dtype.itemsize for o in [*operands, *in_hbm])
    return pl.pallas_call(
        body,
        out_shape=out_shape,
        in_specs=[WHOLE] * len(operands) + [IN_HBM] * len(in_hbm),
        out_specs=[WHOLE] * len(out_shape),
        scratch_shapes=scratch,
        compiler_params=pltpu.CompilerParams(vmem_limit_bytes=limit * 2**20),
        cost_estimate=pl.CostEstimate(flops=flops, bytes_accessed=read, transcendentals=0),
    )(*operands, *in_hbm)


def column_blocks(width):
    block = next(b for b in (512, 256, 128, width) if width % b == 0)
    return [slice(start, start + block) for start in range(0, width, block)]


def row_blocks(values, start, stop):
    return [values[:, at : at + LANES] for at in range(start, stop, LANES)]


def message_body(hidden_in, ids_in, levels_in, gain_in, own_ref, other_ref, gain_ref, hidden, ids, levels, gain, semaphores):
    copies = [
        pltpu.make_async_copy(source, target, semaphores.at[k])
        for k, (source, target) in enumerate(
            [(hidden_in, hidden), (ids_in, ids), (levels_in, levels), (gain_in, gain)]
        )
    ]
    for copy in copies:
        copy.start()
    for copy in copies:
        copy.wait()
    half_width = hidden.shape[1] // 2
    half_rows = half_width // LANES
    is_first = lax.axis_index("expert") % 2 == 0
    row = lax.broadcasted_iota(jnp.int32, own_ref.shape, 0)

    def route_row(ref):
        values = [widened(ref[step]) for step in range(ref.shape[0])]
        used = len(values) * values[0].shape[1]
        return jnp.concatenate(values + [jnp.zeros((1, LANES - used), jnp.float32)], axis=1)

    routing = [route_row(ids), route_row(levels)]
    features = widened(hidden[...])
    first = row_blocks(features, 0, half_width)
    second = row_blocks(features, half_width, 2 * half_width)
    for target, pairs in ((own_ref, zip(first, second)), (other_ref, zip(second, first))):
        message = jnp.zeros(own_ref.shape, jnp.float32)
        for place, values in enumerate([jnp.where(is_first, a, b) for a, b in pairs] + routing):
            message = jnp.where(row == place, values, message)
        target[...] = rounded(message)
    for place in range(half_rows):
        gain_ref[:, place * LANES : (place + 1) * LANES] = jnp.where(
            is_first, gain[place : place + 1], gain[half_rows + place : half_rows + place + 1]
        )


def weights_body(*refs, first, before):
    gate_up_ref, weight_ref, arrived_ref, semaphores = refs[before:]
    part = arrived_ref.shape[2]
    count = semaphores.shape[0]
    block = arrived_ref.shape[0] // count
    blocks = [pl.ds(k * block, block) for k in range(count)]
    copies = [
        pltpu.make_async_copy(
            gate_up_ref.at[pl.ds(first + k * block, block)], arrived_ref.at[rows], semaphores.at[k]
        )
        for k, rows in enumerate(blocks)
    ]
    for copy in copies:
        copy.start()
    for copy, rows in zip(copies, blocks):
        copy.wait()
        weight_ref[rows] = arrived_ref[rows].reshape(block, 2 * part)


def joined_body(piece_count, *refs):
    pieces, out_ref = refs[:piece_count], refs[-1]
    size = out_ref.shape[0] // len(pieces)
    for k, piece in enumerate(pieces):
        out_ref[k * size : (k + 1) * size] = piece[...].reshape(size, *out_ref.shape[1:])


def own_core_of():
    rack, group = lax.axis_index("rack"), lax.axis_index("expert") // 2
    bits = [rack // 2**k for k in range(lax.axis_size("rack").bit_length() - 1)]
    bits += [group // 2**k for k in range(lax.axis_size("expert").bit_length() - 2)]
    return sum(bits) % 2


def own_place_of(core_rows, group_count):
    rack = lax.axis_index("rack")
    return (rack + own_core_of()) % 2 * core_rows + rack // 2 * group_count + lax.axis_index("expert")


def placed(gathered_refs, half_width, rack_count, group_count):
    wide = jnp.concatenate([ref[...].reshape(ref.shape[0], -1) for ref in gathered_refs], axis=0)
    count = wide.shape[0]
    place = lax.broadcasted_iota(jnp.int32, (count, count), 0)
    source = lax.broadcasted_iota(jnp.int32, (count, count), 1)
    near, far = gather_masks(rack_count, group_count)
    distance = source // (count // 2) * (count // 2)
    for masks, index in ((near, source % len(near)), (far, source // len(near) % len(far))):
        for k, (rack, group) in enumerate(masks):
            step = rack % 2 * (count // 2) + rack // 2 * group_count + group
            distance = distance ^ jnp.where(index == k, step, 0)
    own_place = own_place_of(count // 2, group_count)
    to_place = rounded(jnp.where(place == (distance ^ own_place), 1.0, 0.0))
    wide = jnp.dot(to_place, wide, preferred_element_type=jnp.float32)
    residual = wide[:, :half_width]
    ids = wide[:, half_width : half_width + LANES]
    levels = wide[:, half_width + LANES : half_width + 2 * LANES]
    lane = lax.broadcasted_iota(jnp.int32, ids.shape, 1)
    chosen = ids == lax.axis_index("rack").astype(jnp.float32)
    mixing = jnp.zeros(ids.shape, jnp.float32)
    for step in range(STEPS):
        of_step = lane // TOP == step
        total = jnp.sum(jnp.where(of_step, levels, 0.0), axis=1, keepdims=True)
        share = jnp.sum(jnp.where(of_step & chosen, levels / total, 0.0), axis=1, keepdims=True)
        mixing = jnp.where(lane == step, widened(rounded(share)), mixing)
    return residual, mixing


def piece_columns(piece, part):
    size = part // PIECES
    return [slice(start, start + size) for start in (piece * size, part + piece * size)]


def multiplied(scaled, upper_ref, lower_ref, piece, product_ref, message_ref):
    depth, width = upper_ref.shape
    size = width // 2 // PIECES
    for k, columns in enumerate(piece_columns(piece, width // 2)):
        product = jnp.dot(scaled[:, :depth], upper_ref[:, columns], preferred_element_type=jnp.float32)
        product += jnp.dot(scaled[:, depth:], lower_ref[:, columns], preferred_element_type=jnp.float32)
        product_ref[:, k * size : (k + 1) * size] = product
        message_ref[:, k * size : (k + 1) * size] = rounded(product)


def first_piece_body(step, rack_count, group_count, *refs):
    first, last = step == 0, step == STEPS - 1
    if first:
        *gathered_refs, gain_ref, upper_ref, lower_ref, residual_ref, mixing_ref, scaled_ref, product_ref, message_ref = refs
        residual, mixing_ref[...] = placed(gathered_refs, gain_ref.shape[1], rack_count, group_count)
        residual_ref[...] = residual
    else:
        before_ref, own_ref, other_ref, gain_ref, upper_ref, lower_ref, *residual_refs, scaled_ref, product_ref, message_ref = refs
        residual = before_ref[...] + jnp.concatenate([own_ref[...], widened(other_ref[...])], axis=0)
        if last:
            place = lax.broadcasted_iota(jnp.int32, (residual.shape[0], 1), 0)
            own_place = own_place_of(residual.shape[0] // 2, group_count)
            for ref, wanted in zip(residual_refs, (own_place, own_place ^ 1)):
                ref[...] = jnp.sum(jnp.where(place == wanted, residual, 0.0), axis=0, keepdims=True)
        else:
            residual_refs[0][...] = residual
    scaled = rounded(residual * gain_ref[...])
    scaled_ref[...] = scaled
    multiplied(scaled, upper_ref, lower_ref, 0, product_ref, message_ref)
    square_sum = jnp.sum(residual * residual, axis=1, keepdims=True)
    square_high = widened(rounded(square_sum))
    lane = lax.broadcasted_iota(jnp.int32, (residual.shape[0], LANES), 1)
    tail = jnp.where(lane == 0, square_high, square_sum - square_high)
    message_ref[:, product_ref.shape[1] :] = rounded(tail)


def other_piece_body(piece, scaled_ref, upper_ref, lower_ref, product_ref, message_ref):
    multiplied(scaled_ref[...], upper_ref, lower_ref, piece, product_ref, message_ref)


def down_body(step, piece, model_width, group_count, tail_ref, other_tail_ref, product_ref, swapped_ref, mixing_ref, weight_ref, *refs):
    width = product_ref.shape[1]
    size = width // 2
    tails = widened(tail_ref[:, width:]) + widened(other_tail_ref[:, width:])
    square_sum = tails[:, 0:1] + tails[:, 1:2]
    scale = lax.rsqrt(square_sum / model_width + 1e-06)
    whole = product_ref[...] + widened(swapped_ref[:, :width])
    gate = whole[:, :size] * scale
    up = whole[:, size:] * scale
    activated = rounded(gate / (1.0 + jnp.exp(-gate)) * up)
    mixing = mixing_ref[...]
    count = mixing.shape[0]
    last = step == STEPS - 1
    mixing = mixing[:, step : step + 1]
    rows = slice(piece * size, (piece + 1) * size)
    before_refs, out_refs = (refs[:1], refs[1:]) if piece else ((), refs)
    final = piece == PIECES - 1
    for columns in [slice(0, weight_ref.shape[1])] if last and final else column_blocks(weight_ref.shape[1]):
        term = jnp.dot(activated, weight_ref[rows, columns], preferred_element_type=jnp.float32)
        for ref in before_refs:
            term = term + ref[:, columns]
        if not final:
            out_refs[0][:, columns] = term
            continue
        update = widened(rounded(term)) * mixing
        if not last:
            out_refs[0][:, columns] = update[: count // 2]
            out_refs[1][:, columns] = rounded(update[count // 2 :])
            continue
        blocks = rounded(update).reshape(count, -1, LANES)
        for start in range(0, count, group_count):
            chip, core = start % (count // 2) // group_count, (start // (count // 2) + own_core_of()) % 2
            out_refs[0][pl.ds((2 * chip + core) * group_count, group_count)] = blocks[start : start + group_count]


def result_body(arrived_ref, own_ref, other_ref, out_ref):
    count, half_width = arrived_ref.shape[0], own_ref.shape[1]
    terms = widened(arrived_ref[...].reshape(count, half_width))
    of_first = lax.broadcasted_iota(jnp.int32, (count, 1), 0) % 2 == 0
    is_first = lax.axis_index("expert") % 2 == 0
    own, other = own_ref[...], other_ref[...]
    out_ref[:, :half_width] = jnp.where(is_first, own, other) + jnp.sum(
        jnp.where(of_first, terms, 0.0), axis=0, keepdims=True
    )
    out_ref[:, half_width:] = jnp.where(is_first, other, own) + jnp.sum(
        jnp.where(of_first, 0.0, terms), axis=0, keepdims=True
    )


def dense_steps(hidden_in, norm_gain, expert_ids, gate_levels, w_gate_up, w_down):
    rack_count = lax.axis_size("rack")
    group_count = lax.axis_size("expert")
    core_rows = rack_count // 2 * group_count
    token_count = 2 * core_rows
    model_width = hidden_in.shape[1]
    half_width = model_width // 2
    part_width = w_down.shape[2]
    product_width = 2 * part_width
    product_flops = 2 * token_count * half_width * product_width

    block_shape = (half_width // LANES + 2, LANES)
    sources = [hidden_in, expert_ids, gate_levels, norm_gain.reshape(-1, LANES)]
    own, other, gain_half = kernel_call(
        message_body,
        [
            in_vmem(block_shape, jnp.bfloat16),
            in_vmem(block_shape, jnp.bfloat16),
            in_vmem((1, half_width), jnp.float32),
        ],
        [],
        in_hbm=sources,
        scratch=[*(in_vmem(a.shape, a.dtype) for a in sources), pltpu.SemaphoreType.DMA((len(sources),))],
    )
    block = next(b for b in (128, 16, half_width) if half_width % b == 0)

    def turned(start, stop, *before):
        return kernel_call(
            functools.partial(weights_body, first=start, before=len(before)),
            [in_vmem((stop - start, product_width), jnp.bfloat16)],
            before,
            in_hbm=[w_gate_up[0, 0]],
            scratch=[
                in_vmem((stop - start, 2, part_width), jnp.bfloat16),
                pltpu.SemaphoreType.DMA(((stop - start) // block,)),
            ],
            limit=12,
        )[0]

    def joined(pieces, count, *before):
        out_shape = [in_vmem((count,) + block_shape, jnp.bfloat16)]
        return kernel_call(functools.partial(joined_body, len(pieces)), out_shape, [*pieces, *before])[0]

    near, far = gather_masks(rack_count, group_count)
    middle = -(-half_width // 2 // 256) * 256
    upper = turned(0, middle)
    rows = [own] + [exchanged_both(other if group else own, rack, group) for rack, group in near[1:]]
    rows = joined(rows, len(near), upper)
    lower = turned(middle, half_width, rows)
    gate_up_weights = [upper, lower]
    rows = [rows] + [exchanged_both(rows, rack, group) for rack, group in far[1:]]
    rows = joined(rows, core_rows, lower)
    gathered = [rows, exchanged(rows, "rack", 1)]

    piece_width = product_width // PIECES
    for step_index in range(STEPS):
        last = step_index == STEPS - 1
        product_shape = in_vmem((token_count, piece_width), jnp.float32)
        kept = [in_vmem((token_count, half_width), jnp.float32)]
        if step_index == 0:
            operands = gathered
            kept += [in_vmem((token_count, LANES), jnp.float32)]
        else:
            operands = [residual, update, received]
        if last:
            kept = [in_vmem((1, half_width), jnp.float32)] * 2
        *kept, scaled, product, message = kernel_call(
            functools.partial(first_piece_body, step_index, rack_count, group_count),
            [
                *kept,
                in_vmem((token_count, half_width), jnp.bfloat16),
                product_shape,
                in_vmem((token_count, piece_width + LANES), jnp.bfloat16),
            ],
            operands + [gain_half, *gate_up_weights],
            product_flops // PIECES,
        )
        if step_index == 0:
            residual, mixing = kept
        else:
            residual = kept[0]
        products, swapped = [product], [exchanged(message, "expert", 1)]
        for piece in range(1, PIECES):
            product, piece_message = kernel_call(
                functools.partial(other_piece_body, piece),
                [product_shape, in_vmem((token_count, piece_width), jnp.bfloat16)],
                [scaled, *gate_up_weights],
                product_flops // PIECES,
            )
            products.append(product)
            swapped.append(exchanged(piece_message, "expert", 1))
        if last:
            own_row, other_row = kept
            other_row = exchanged(other_row, "expert", 1)
        updates = []
        for piece in range(PIECES):
            if piece < PIECES - 1:
                shapes = [in_vmem((token_count, half_width), jnp.float32)]
            elif last:
                shapes = [in_vmem((token_count, half_width // LANES, LANES), jnp.bfloat16)]
            else:
                shapes = [
                    in_vmem((core_rows, half_width), jnp.float32),
                    in_vmem((core_rows, half_width), jnp.bfloat16),
                ]
            updates = kernel_call(
                functools.partial(down_body, step_index, piece, model_width, group_count),
                shapes,
                [message, swapped[0], products[piece], swapped[piece], mixing, w_down[0, 0], *updates],
                product_flops // 2 // PIECES,
            )
        if last:
            updates = lax.optimization_barrier((updates[0], other_row))
            break
        update = updates[0] + widened(exchanged(updates[1], "rack", 1))
        sent = rounded(update)
        for mask in range(2, rack_count, 2):
            update = update + widened(exchanged_both(sent, *crossed(mask, 0)))
        sent = rounded(update)
        for mask in range(2, group_count, 2):
            update = update + widened(exchanged_both(sent, *crossed(0, mask)))
        received = exchanged(rounded(update), "rack", 1)

    arrived = lax.all_to_all(updates[0], ("rack", "expert"), split_axis=0, concat_axis=0, tiled=True)
    (result,) = kernel_call(
        result_body, [jax.ShapeDtypeStruct((1, model_width), jnp.float32)], [arrived, own_row, updates[1]]
    )
    return result


def per_device(hidden_in, norm_gain, expert_ids, gate_levels, w_gate_up, w_down):
    rack_count = lax.axis_size("rack")
    group_count = lax.axis_size("expert")
    group_index = lax.axis_index("expert")
    half_index = group_index % 2
    tok_rows = hidden_in.shape[0]
    rack_rows = tok_rows * group_count
    slot_count = min(rack_rows, 3 * rack_rows * TOP // (2 * rack_count))
    model_width = hidden_in.shape[1]
    half_width = model_width // 2
    part_width = w_down.shape[2]
    gate_up_weight = w_gate_up[0, 0].reshape(half_width, 2 * part_width)
    down_weight = w_down[0, 0]
    all_ids, all_levels = (
        lax.all_gather(expert_ids, "expert", axis=1, tiled=True),
        lax.all_gather(gate_levels, "expert", axis=1, tiled=True),
    )
    expert_range = jnp.arange(rack_count, dtype=jnp.int32)
    slot_ids = jnp.arange(slot_count, dtype=jnp.int32)
    residual = hidden_in.astype(jnp.float32)
    for step_index in range(STEPS):
        mean_square = jnp.mean(residual * residual, axis=-1, keepdims=True)
        normed = (residual * lax.rsqrt(mean_square + 1e-06) * norm_gain).astype(jnp.bfloat16)
        rack_normed = lax.all_gather(normed, "expert", axis=0, tiled=True)
        picked = all_ids[step_index]
        level_vals = all_levels[step_index].astype(jnp.float32)
        shares = level_vals / jnp.sum(level_vals, axis=-1, keepdims=True)
        matches = picked[:, :, None] == expert_range[None, None, :]
        chosen = jnp.sum(matches.astype(jnp.int32), axis=1)
        mixing = jnp.sum(jnp.where(matches, shares[:, :, None], jnp.float32(0.0)), axis=1).astype(
            jnp.bfloat16
        )
        slot_rank = jnp.cumsum(chosen, axis=0) - chosen
        placement = chosen[:, :, None] * (slot_rank[:, :, None] == slot_ids).astype(jnp.int32)
        dispatch_map = (
            jnp.transpose(placement, (1, 2, 0))
            .reshape(rack_count * slot_count, rack_rows)
            .astype(jnp.bfloat16)
        )
        outgoing = jnp.dot(dispatch_map, rack_normed, preferred_element_type=jnp.float32).astype(
            jnp.bfloat16
        )
        outgoing = outgoing.reshape(rack_count, slot_count, model_width)
        combine_map = (placement.astype(jnp.bfloat16) * mixing[:, :, None]).reshape(
            rack_rows, rack_count * slot_count
        )
        half_rows = lax.dynamic_slice_in_dim(outgoing, half_index * half_width, half_width, 2)
        slot_rows = lax.all_to_all(half_rows, "rack", split_axis=0, concat_axis=0, tiled=True)
        layout = slot_rows.shape
        flat_rows = slot_rows.reshape(-1, half_width)
        gate_up = jnp.dot(flat_rows, gate_up_weight, preferred_element_type=jnp.float32)
        gate_up = gate_up + swapped(gate_up.astype(jnp.bfloat16), "expert", 0).astype(gate_up.dtype)
        activated = (jax.nn.silu(gate_up[:, :part_width]) * gate_up[:, part_width:]).astype(
            jnp.bfloat16
        )
        partial_value = jnp.dot(activated, down_weight, preferred_element_type=jnp.float32).astype(
            jnp.bfloat16
        )
        partial_value = partial_value.reshape(layout)
        finished = lax.all_to_all(partial_value, "rack", split_axis=0, concat_axis=0, tiled=True)
        partial_sum = jnp.dot(
            combine_map, finished.reshape(-1, half_width), preferred_element_type=jnp.float32
        )
        full_sum = jnp.zeros((rack_rows, model_width), jnp.float32)
        full_sum = lax.dynamic_update_slice_in_dim(
            full_sum, partial_sum, half_index * half_width, 1
        )
        update = lax.psum_scatter(
            full_sum.astype(jnp.bfloat16), "expert", scatter_dimension=0, tiled=True
        ).astype(jnp.float32)
        residual = residual + update
    return residual


def solution(mesh):
    in_specs = (
        P(("rack", "expert"), None),
        P(),
        P(None, ("rack", "expert"), None),
        P(None, ("rack", "expert"), None),
        P("rack", "expert", None, None, None),
        P("rack", "expert", None, None),
    )
    out_specs = P(("rack", "expert"), None)
    dense = mesh.shape["rack"] <= TOP
    return jax.shard_map(
        dense_steps if dense else per_device, mesh=mesh, in_specs=in_specs, out_specs=out_specs, check_vma=False
    )
```
